128 devices in a mesh: wave: 32 (over z, y, core), lev: 4 (over x).
Axes of the slice: x: 4, y: 4, z: 4, core: 2. Of those that a mesh axis runs over, the one named last changes fastest.
Arguments:
- grid_adjoint: bfloat16 [3, 16, 128, 1536], P(None, 'lev', 'wave'), may hold values from -6 to 6
- courant: bfloat16 [16, 128, 1536], P('lev', 'wave'), may hold values from -0.8984375 to 0.8984375
- row_points: int32 [128], P('wave'), may hold values from 20 to 1536, as said below
- wave_order: int32 [512], replicated, may hold values from 0 to 511, as said below
- legendre: bfloat16 [512, 512, 128], P('wave', 'lev'), may hold values from -0.013671875 to 0.013671875
- vert_inverse: float32 [3, 16, 16], replicated, as said below
Outputs:
- spectral_adjoint: float32 [3, 16, 512, 2, 512], P(None, None, ('wave', 'lev'))
The draws below stay inside these ranges and needn't reach their ends.
Inputs may be any that keep to these rules, and one draw needn't show every extreme that they name: Row j has row_points[j] grid points; positions at or beyond it are unused. `wave_order`: A permutation of the wavenumbers 0 to 511 in which slots 2 i and 2 i + 1 hold wavenumbers that sum to 511. `vert_inverse`: each field's matrix has diagonal entries between 0.5 and 2 plus a dense coupling of independent entries.
All inputs are finite; a program needn't handle non-finite values.
Results may differ from the reference program's by a relative error of at most 0.0047.
Values may be sent and summed in bfloat16 or wider, within the bound.
A program may use at most 64 MiB of HBM per device.

```python
import math
import jax
import jax.numpy as jnp
from jax import lax

NLON = 1536
M = 512
LEV = 16
NLAT = 128


def draw_row_points(key, part):
    latitude = jnp.arange(NLAT, dtype=jnp.int32)
    distance = jnp.minimum(latitude, NLAT - 1 - latitude)
    extra = jax.random.randint(jax.random.fold_in(key, 11), (NLAT,), 0, 8, dtype=jnp.int32)
    return jnp.minimum(NLON, 20 + (2 * distance + extra) * NLON // NLAT).astype(jnp.int32)


def draw_wave_order(key, part):
    lower = jax.random.permutation(jax.random.fold_in(key, 23), M // 2).astype(jnp.int32)
    paired = jnp.stack([lower, M - 1 - lower], axis=1)
    return paired.reshape(M).astype(jnp.int32)


def draw_vert_inverse(key, part):
    first_key, second_key = jax.random.split(jax.random.fold_in(key, 37))
    diagonal = jnp.exp(jax.random.uniform(first_key, (3, LEV), jnp.float32, jnp.log(0.5), jnp.log(2.0)))
    coupling = jax.random.normal(second_key, (3, LEV, LEV), jnp.float32) * (0.5 / jnp.sqrt(LEV * 1.0))
    identity = jnp.eye(LEV, dtype=jnp.float32)
    return (coupling + identity[None] * diagonal[:, :, None]).astype(jnp.float32)


def steps_of(own_key, extent, cuts, smallest, high):
    gain, own = 1.0, jax.random.fold_in(own_key, 6)
    for axis_at, blocks in cuts:
        draws = jnp.exp(jax.random.uniform(jax.random.fold_in(own, axis_at), (blocks,), jnp.float32, smallest / len(cuts), high / len(cuts)))
        gain = gain * jnp.repeat(draws, extent[axis_at] // blocks).reshape([-1 if axis == axis_at else 1 for axis in range(len(extent))])
    return gain


def centred(key, shape, scale, most, shards=(), kind=jnp.bfloat16):
    drawn = jax.random.normal(key, shape, jnp.float32) * scale
    if len(shards) > 0:
        drawn = steps_of(key, shape, shards, -0.22, 0.18) * drawn
    return jnp.clip(drawn, min=-most, max=most).astype(kind)


def setup_inputs(seed: int = 0) -> dict:
    seeds = jax.random.split(jax.random.key(seed), 7)
    return {
        "grid_adjoint": centred(seeds[0], (3, LEV, NLAT, NLON), 1.0, 6.0, ((1, 4), (2, 32))),
        "courant": jnp.clip(jax.random.uniform(seeds[1], (LEV, NLAT, NLON), jnp.float32, -0.8984375, 0.8984375) * steps_of(seeds[1], (LEV, NLAT, NLON), ((0, 4), (1, 32)), -0.4, 0.0), -0.8984375, 0.8984375).astype(jnp.bfloat16),
        "row_points": draw_row_points(jax.random.fold_in(seeds[6], 71), 0),
        "wave_order": draw_wave_order(jax.random.fold_in(seeds[6], 71), 0),
        "legendre": centred(seeds[4], (M, M, NLAT), (NLAT * NLON) ** -0.5, 0.013671875, ((0, 32), (1, 4))),
        "vert_inverse": draw_vert_inverse(jax.random.fold_in(seeds[6], 71), 0),
    }


TWO_PI = 2.0 * math.pi


def advect(grid_rows, wind_rows, points):
    row_width = grid_rows.shape[-1]
    positions = jnp.arange(row_width, dtype=jnp.int32)
    counts = points[:, None]
    inside = positions[None, :] < counts
    at_end = positions[None, :] == counts - 1
    mass_flux = jnp.where(inside, wind_rows.astype(jnp.float32)[None] * grid_rows.astype(jnp.float32), 0.0)
    first_flux = mass_flux[..., :1]
    last_flux = jnp.sum(jnp.where(at_end, mass_flux, 0.0), axis=-1, keepdims=True)
    forward_flux = jnp.where(at_end, first_flux, jnp.roll(mass_flux, -1, axis=-1))
    backward_flux = jnp.where(positions == 0, last_flux, jnp.roll(mass_flux, 1, axis=-1))
    result = jnp.where(inside, grid_rows.astype(jnp.float32) + 0.5 * (forward_flux - backward_flux), 0.0)
    return result.astype(jnp.bfloat16)


def fourier_table(points, orders, row_width):
    positions = jnp.arange(row_width, dtype=jnp.int32)
    counts = points[:, None, None]
    phase_index = (orders[None, None, :] * positions[None, :, None]) % counts
    angles = phase_index.astype(jnp.float32) * (TWO_PI / counts.astype(jnp.float32))
    highest = (counts - 1) // 2
    factor = jnp.where(orders[None, None, :] > highest, 0.0, jnp.where(orders[None, None, :] == 0, 1.0, 2.0)).astype(jnp.float32)
    cosines = jnp.stack([jnp.cos(angles) * factor, -jnp.sin(angles) * factor], axis=-1)
    return cosines.reshape(points.shape[0], row_width, 2 * orders.shape[0]).astype(jnp.bfloat16)


def reference(grid_adjoint, courant, row_points, wave_order, legendre, vert_inverse):
    fields, levels, row_count, row_width = grid_adjoint.shape
    row_group = math.gcd(4, row_count)

    def row_block(start):
        grid_rows = lax.dynamic_slice_in_dim(grid_adjoint, start, row_group, 2)
        wind_rows = lax.dynamic_slice_in_dim(courant, start, row_group, 1)
        points = lax.dynamic_slice_in_dim(row_points, start, row_group, 0)
        advected = advect(grid_rows, wind_rows, points)
        cosines = fourier_table(points, wave_order, row_width)
        return jnp.einsum('flgk,gkc->gflc', advected.astype(jnp.float32), cosines.astype(jnp.float32))

    starts = jnp.arange(0, row_count, row_group, dtype=jnp.int32)
    fourier = lax.map(row_block, starts)
    fourier = fourier.reshape(row_count, fields, levels, -1).astype(jnp.bfloat16)
    fourier = jnp.transpose(fourier, (2, 1, 3, 0))
    wave_total = wave_order.shape[0]
    slot_group = math.gcd(16, wave_total)
    degrees = jnp.arange(wave_total, dtype=jnp.int32)

    def wave_block(start):
        fourier_part = lax.dynamic_slice_in_dim(fourier, start * 2, slot_group * 2, 2)
        fourier_part = fourier_part.reshape(levels * fields, slot_group, 2, row_count)
        legendre_rows = lax.dynamic_slice_in_dim(legendre, start, slot_group, 0)
        orders = lax.dynamic_slice_in_dim(wave_order, start, slot_group, 0)
        masked = jnp.where(degrees[None, :, None] >= orders[:, None, None], legendre_rows, jnp.zeros((), legendre_rows.dtype))
        partial_value = jnp.einsum('picj,inj->ipcn', fourier_part.astype(jnp.float32), masked.astype(jnp.float32))
        partial_value = partial_value.reshape(slot_group, levels, fields, 2, wave_total)
        return jnp.einsum('fpl,ipfcn->flicn', vert_inverse, partial_value, precision=lax.Precision.HIGHEST)

    results = lax.map(wave_block, jnp.arange(0, wave_total, slot_group, dtype=jnp.int32))
    results = jnp.transpose(results, (1, 2, 0, 3, 4, 5))
    return results.reshape(fields, levels, wave_total, 2, wave_total)
```

```python
import functools

import jax
import jax.numpy as jnp
from jax import lax
from jax.experimental import pallas as pl
from jax.experimental.pallas import tpu as pltpu
from jax.sharding import PartitionSpec as P

F32 = jnp.float32
BF16 = jnp.bfloat16
MESH = pl.DeviceIdType.MESH
NT = (((1,), (1,)), ((), ()))

SIN_PI = (3.1415927410125732, -5.167712688446045, 2.5501632690429688,
          -0.5992521643638611, 0.08205024898052216, -0.007028118707239628)
COS_PI = (1.0, -4.934802055358887, 4.058709144592285,
          -1.3352118730545044, 0.2349366992712021, -0.024395223706960678)


def horner(coefficients, z):
    value = jnp.full(z.shape, coefficients[-1], F32)
    for c in coefficients[-2::-1]:
        value = value * z + c
    return value


def unit_circle(steps, orders, count):
    inverse = 1.0 / count
    product = steps * orders
    turns = jnp.floor(product * inverse + 0.5)
    x = (product - turns * count) * inverse
    z = x * x
    s = x * horner(SIN_PI, z)
    c = horner(COS_PI, z)
    return 1.0 - 2.0 * s * s, -2.0 * s * c


def iota(shape, axis):
    return lax.broadcasted_iota(jnp.int32, shape, axis)


def advect(grid_ref, wind_ref, points_ref, rows_ref):
    fields, levels, rows, width = grid_ref.shape
    row = iota((rows, width), 0)
    count = jnp.full((rows, width), points_ref[0], jnp.int32)
    for j in range(1, rows):
        count = jnp.where(row == j, points_ref[j], count)
    position = iota((rows, width), 1)
    inside = position < count
    at_end = position == count - 1
    at_start = position == 0
    for level in range(levels):
        wind = wind_ref[level].astype(F32)
        for field in range(fields):
            grid = grid_ref[field, level].astype(F32)
            flux = jnp.where(inside, wind * grid, 0.0)
            first = flux[:, :1]
            last = jnp.sum(jnp.where(at_end, flux, 0.0), axis=1, keepdims=True)
            forward = jnp.where(at_end, first, pltpu.roll(flux, width - 1, 1))
            backward = jnp.where(at_start, last, pltpu.roll(flux, 1, 1))
            result = jnp.where(inside, grid + 0.5 * (forward - backward), 0.0)
            at = rows * (field * levels + level)
            for k1 in range(width // 128):
                rows_ref[k1, at:at + rows, :] = result[:, 128 * k1:128 * (k1 + 1)]
    used = rows * fields * levels
    rows_ref[:, used:, :] = jnp.zeros((rows_ref.shape[0], rows_ref.shape[1] - used, 128), F32)


def column_orders(orders_ref):
    slots = orders_ref.shape[1]
    orders = orders_ref[...].astype(F32)
    high = jnp.floor(orders * 0.5)
    low = orders - 2.0 * high
    pick = (iota((slots, slots), 0) == 4 * (iota((slots, slots), 1) % 128)
            + iota((slots, slots), 1) // 128).astype(F32).astype(BF16)
    pair = jnp.concatenate([high, low, jnp.zeros((6, slots), F32)], axis=0).astype(BF16)
    moved = jnp.dot(pair, pick, preferred_element_type=F32)
    return 2.0 * moved[0:1] + moved[1:2]


def row_transform(j, points_ref, orders, rows_ref, pages_ref):
    blocks = rows_ref.shape[0]
    slots = orders.shape[1]
    count = jnp.full((1, slots), points_ref[j], jnp.int32).astype(F32)
    fine_cos, fine_sin = unit_circle(iota((16, 1), 0).astype(F32), orders, count)
    mid_cos, mid_sin = unit_circle(16.0 * iota((8, 1), 0).astype(F32), orders, count)
    far_cos, far_sin = unit_circle(128.0 * iota((16, 1), 0).astype(F32), orders, count)
    weight = jnp.where(2.0 * orders >= count, 0.0, jnp.where(orders == 0.0, 1.0, 2.0))
    far_cos = far_cos * weight
    far_sin = far_sin * weight
    left = jnp.concatenate(
        [rows_ref[k1, pl.ds(j, 16, stride=4), :] for k1 in range(blocks)], axis=0
    ).astype(BF16)
    stacked = []
    for i in range(slots // 128):
        own = slice(128 * i, 128 * (i + 1))
        c0, s0 = fine_cos[:, own], fine_sin[:, own]
        real, imag = [], []
        for b in range(8):
            c1, s1 = mid_cos[b:b + 1, own], mid_sin[b:b + 1, own]
            real.append(c1 * c0 - s1 * s0)
            imag.append(c1 * s0 + s1 * c0)
        table = jnp.concatenate(
            [jnp.concatenate(real, axis=0), jnp.concatenate(imag, axis=0)], axis=1
        ).astype(BF16)
        partial = jnp.dot(left, table, preferred_element_type=F32)
        total_real = jnp.zeros((16, 128), F32)
        total_imag = jnp.zeros((16, 128), F32)
        for k1 in range(blocks):
            u = partial[16 * k1:16 * (k1 + 1), :128]
            v = partial[16 * k1:16 * (k1 + 1), 128:]
            c2, s2 = far_cos[k1:k1 + 1, own], far_sin[k1:k1 + 1, own]
            total_real = total_real + (c2 * u - s2 * v)
            total_imag = total_imag + (c2 * v + s2 * u)
        stacked += [total_real, total_imag]
    pages_ref[pl.ds(128 * j, 128), :] = jnp.transpose(jnp.concatenate(stacked, axis=0))


def vertical_table(vert_ref):
    fields, levels, _ = vert_ref.shape
    spread = (iota((2 * levels, levels), 0) // 2 == iota((2 * levels, levels), 1)).astype(F32)
    rows = jnp.concatenate(
        [lax.dot_general(spread, vert_ref[f], NT, precision=lax.Precision.HIGHEST,
                         preferred_element_type=F32) for f in range(fields)], axis=0)
    column = iota((levels, 512), 1)
    pick = (iota((levels, 512), 0) == 4 * (column // 128) + column % 4).astype(F32)
    block = jnp.dot(rows, pick, precision=lax.Precision.HIGHEST, preferred_element_type=F32)
    shape = block.shape
    row, column = iota(shape, 0), iota(shape, 1)
    keep = (row // (2 * levels) == column // 4 % 4) & (row % 2 == column // 16 % 2)
    block = jnp.where(keep, block, 0.0)
    slot = column // 32 % 4
    return jnp.concatenate([jnp.where(slot == i, block, 0.0) for i in range(4)], axis=0)


def finish(first_slot, order_ref, vert, pages_ref, joined_ref, table_ref, out_ref):
    sources, rows, _ = pages_ref.shape
    for s in range(sources):
        joined_ref[rows * s:rows * (s + 1), :] = pages_ref[s].astype(F32)
    high = vert.astype(BF16)
    low = (vert - high.astype(F32)).astype(BF16)
    mixed = None
    for v in range(4):
        block = joined_ref[128 * v:128 * (v + 1), :].astype(BF16)
        own = slice(128 * v, 128 * (v + 1))
        for part in (high, low):
            term = lax.dot_general(part[:, own], block, NT, preferred_element_type=F32)
            mixed = term if mixed is None else mixed + term
    mixed_high = mixed.astype(BF16)
    mixed_low = (mixed - mixed_high.astype(F32)).astype(BF16)
    both = jnp.concatenate([mixed_high, mixed_low], axis=1)
    fields, levels = out_ref.shape[0], out_ref.shape[1]
    lines = fields * levels * 2
    for i in range(4):
        table = jnp.concatenate([table_ref[v, i] for v in range(4)], axis=0)
        table = jnp.concatenate([table, table], axis=1)
        summed = lax.dot_general(both[lines * i:lines * (i + 1)], table, NT,
                                 preferred_element_type=F32)
        degree = iota(summed.shape, 1)
        summed = jnp.where(degree >= order_ref[first_slot + i], summed, 0.0)
        for q in range(fields * levels):
            out_ref[q // levels, q % levels, i] = summed[2 * q:2 * q + 2]


def kernel(waves, levs, grid_ref, wind_ref, points_ref, order_ref, orders_ref, legendre_ref,
           vert_ref, out_ref, rows_ref, pages_ref, send_ref, recv_ref, joined_ref, table_ref,
           send_sem, recv_sem, table_send_sem, table_recv_sem, local_sem):
    w, v = lax.axis_index("wave"), lax.axis_index("lev")
    devices = waves * levs
    me = w * levs + v
    barrier = pltpu.get_barrier_semaphore()

    def greet(step, carry):
        d = lax.rem(me + step, devices)
        pl.semaphore_signal(barrier, inc=1, device_id=(d // levs, lax.rem(d, levs)),
                            device_id_type=MESH)
        return carry

    lax.fori_loop(1, devices, greet, 0)
    advect(grid_ref, wind_ref, points_ref, rows_ref)
    orders = column_orders(orders_ref)
    pl.semaphore_wait(barrier, devices - 1)

    own_table = pltpu.make_async_copy(
        legendre_ref.at[pl.ds(4 * v, 4)], table_ref.at[v], local_sem.at[0])
    own_table.start()
    table_copies = []
    for step in range(1, levs):
        u = lax.rem(v + step, levs)
        copy = pltpu.make_async_remote_copy(
            src_ref=legendre_ref.at[pl.ds(4 * u, 4)], dst_ref=table_ref.at[v],
            send_sem=table_send_sem.at[step - 1], recv_sem=table_recv_sem.at[step - 1],
            device_id=(w, u), device_id_type=MESH)
        copy.start()
        table_copies.append(copy)

    for j in range(4):
        row_transform(j, points_ref, orders, rows_ref, pages_ref)

    slot = waves * v + w

    def pack(d):
        send_ref[d] = pages_ref[pl.ds(d, 4, stride=128), :].astype(BF16)

    pack(me)
    own_page = pltpu.make_async_copy(send_ref.at[me], recv_ref.at[slot], local_sem.at[1])
    own_page.start()

    def send(step, carry):
        d = lax.rem(me + step, devices)
        pack(d)
        pltpu.make_async_remote_copy(
            src_ref=send_ref.at[d], dst_ref=recv_ref.at[slot], send_sem=send_sem,
            recv_sem=recv_sem, device_id=(d // levs, lax.rem(d, levs)), device_id_type=MESH,
        ).start()
        return carry

    lax.fori_loop(1, devices, send, 0)
    vert = vertical_table(vert_ref)
    own_table.wait()
    for copy in table_copies:
        copy.wait()
    own_page.wait()
    every = pltpu.make_async_remote_copy(
        src_ref=send_ref.at[pl.ds(0, devices - 1)], dst_ref=recv_ref.at[pl.ds(0, devices - 1)],
        send_sem=send_sem, recv_sem=recv_sem,
        device_id=(w, lax.rem(v + 1, levs)), device_id_type=MESH)
    every.wait_recv()
    every.wait_send()
    finish(4 * me, order_ref, vert, recv_ref, joined_ref, table_ref, out_ref)


def body(grid_adjoint, courant, row_points, wave_order, legendre, vert_inverse, *, waves, levs):
    fields, levels, rows, width = grid_adjoint.shape
    slots = legendre.shape[0] // levs
    degrees = legendre.shape[1] * levs
    devices = waves * levs
    vmem = pl.BlockSpec(memory_space=pltpu.VMEM)
    smem = pl.BlockSpec(memory_space=pltpu.SMEM)
    return pl.pallas_call(
        functools.partial(kernel, waves, levs),
        out_shape=jax.ShapeDtypeStruct((fields, levels * levs, slots, 2, degrees), F32),
        in_specs=[vmem, vmem, smem, smem, vmem, pl.BlockSpec(memory_space=pl.ANY), vmem],
        out_specs=vmem,
        scratch_shapes=[
            pltpu.VMEM((width // 128, 64, 128), F32),
            pltpu.VMEM((rows * 128, 128), F32),
            pltpu.VMEM((devices, 4, 128), BF16),
            pltpu.VMEM((devices, 4, 128), BF16),
            pltpu.VMEM((512, 128), F32),
            pltpu.VMEM((levs, slots) + legendre.shape[1:], BF16),
            pltpu.SemaphoreType.DMA,
            pltpu.SemaphoreType.DMA,
            pltpu.SemaphoreType.DMA((levs - 1,)),
            pltpu.SemaphoreType.DMA((levs - 1,)),
            pltpu.SemaphoreType.DMA((2,)),
        ],
        compiler_params=pltpu.CompilerParams(
            collective_id=0, has_side_effects=True, vmem_limit_bytes=40 * 2**20),
    )(grid_adjoint, courant, row_points, wave_order, wave_order.reshape(1, -1), legendre,
      vert_inverse)


def solution(mesh):
    return jax.shard_map(
        functools.partial(body, waves=mesh.shape["wave"], levs=mesh.shape["lev"]),
        mesh=mesh,
        in_specs=(
            P(None, "lev", "wave", None),
            P("lev", "wave", None),
            P("wave"),
            P(),
            P("wave", "lev", None),
            P(),
        ),
        out_specs=P(None, None, ("wave", "lev"), None, None),
        check_vma=False,
    )
```

```python
import functools

import jax
import jax.numpy as jnp
from jax import lax
from jax.experimental import pallas as pl
from jax.experimental.pallas import tpu as pltpu
from jax.sharding import PartitionSpec as P

F32 = jnp.float32
BF16 = jnp.bfloat16
MESH = pl.DeviceIdType.MESH
NT = (((1,), (1,)), ((), ()))

SIN_PI = (3.1415927410125732, -5.167712688446045, 2.5501632690429688,
          -0.5992521643638611, 0.08205024898052216, -0.007028118707239628)
COS_PI = (1.0, -4.934802055358887, 4.058709144592285,
          -1.3352118730545044, 0.2349366992712021, -0.024395223706960678)


def horner(coefficients, z):
    value = jnp.full(z.shape, coefficients[-1], F32)
    for c in coefficients[-2::-1]:
        value = value * z + c
    return value


def unit_circle(steps, orders, count):
    inverse = 1.0 / count
    product = steps * orders
    turns = jnp.floor(product * inverse + 0.5)
    x = (product - turns * count) * inverse
    z = x * x
    s = x * horner(SIN_PI, z)
    c = horner(COS_PI, z)
    return 1.0 - 2.0 * s * s, -2.0 * s * c


def iota(shape, axis):
    return lax.broadcasted_iota(jnp.int32, shape, axis)


def advect(grid_ref, wind_ref, points_ref, rows_ref):
    fields, levels, rows, width = grid_ref.shape
    shape = (2 * rows, width)
    row = iota(shape, 0) % rows
    count = jnp.full(shape, points_ref[0], jnp.int32)
    for j in range(1, rows):
        count = jnp.where(row == j, points_ref[j], count)
    position = iota(shape, 1)
    inside = position < count
    at_end = position == count - 1
    at_start = position == 0

    def pair(ref, *at):
        return jnp.concatenate(
            [ref[(*at[:-1], at[-1] + half)].astype(F32) for half in range(2)], axis=0)

    for level in range(0, levels, 2):
        wind = pair(wind_ref, level)
        for field in range(fields):
            grid = pair(grid_ref, field, level)
            flux = jnp.where(inside, wind * grid, 0.0)
            first = flux[:, :1]
            last = jnp.sum(jnp.where(at_end, flux, 0.0), axis=1, keepdims=True)
            forward = jnp.where(at_end, first, pltpu.roll(flux, width - 1, 1))
            backward = jnp.where(at_start, last, pltpu.roll(flux, 1, 1))
            result = jnp.where(inside, grid + 0.5 * (forward - backward), 0.0)
            at = rows * (field * levels + level)
            for k1 in range(width // 128):
                rows_ref[k1, at:at + 2 * rows, :] = result[:, 128 * k1:128 * (k1 + 1)]
    used = rows * fields * levels
    rows_ref[:, used:, :] = jnp.zeros((rows_ref.shape[0], rows_ref.shape[1] - used, 128), F32)


def column_orders(orders_ref):
    slots = orders_ref.shape[1]
    orders = orders_ref[...].astype(F32)
    high = jnp.floor(orders * 0.5)
    low = orders - 2.0 * high
    pick = (iota((slots, slots), 0) == 4 * (iota((slots, slots), 1) % 128)
            + iota((slots, slots), 1) // 128).astype(F32).astype(BF16)
    pair = jnp.concatenate([high, low, jnp.zeros((6, slots), F32)], axis=0).astype(BF16)
    moved = jnp.dot(pair, pick, preferred_element_type=F32)
    return 2.0 * moved[0:1] + moved[1:2]


def row_transform(j, points_ref, orders, rows_ref, pages_ref):
    blocks = rows_ref.shape[0]
    slots = orders.shape[1]
    count = jnp.full((1, slots), points_ref[j], jnp.int32).astype(F32)
    fine_cos, fine_sin = unit_circle(iota((16, 1), 0).astype(F32), orders, count)
    mid_cos, mid_sin = unit_circle(16.0 * iota((8, 1), 0).astype(F32), orders, count)
    far_cos, far_sin = unit_circle(128.0 * iota((16, 1), 0).astype(F32), orders, count)
    weight = jnp.where(2.0 * orders >= count, 0.0, jnp.where(orders == 0.0, 1.0, 2.0))
    far_cos = far_cos * weight
    far_sin = far_sin * weight
    left = jnp.concatenate(
        [rows_ref[k1, pl.ds(j, 16, stride=4), :] for k1 in range(blocks)], axis=0
    ).astype(BF16)
    stacked = []
    for i in range(slots // 128):
        own = slice(128 * i, 128 * (i + 1))
        c0, s0 = fine_cos[:, own], fine_sin[:, own]
        real, imag = [], []
        for b in range(8):
            c1, s1 = mid_cos[b:b + 1, own], mid_sin[b:b + 1, own]
            real.append(c1 * c0 - s1 * s0)
            imag.append(c1 * s0 + s1 * c0)
        table = jnp.concatenate(
            [jnp.concatenate(real, axis=0), jnp.concatenate(imag, axis=0)], axis=1
        ).astype(BF16)
        partial = jnp.dot(left, table, preferred_element_type=F32)
        total_real = jnp.zeros((16, 128), F32)
        total_imag = jnp.zeros((16, 128), F32)
        for k1 in range(blocks):
            u = partial[16 * k1:16 * (k1 + 1), :128]
            v = partial[16 * k1:16 * (k1 + 1), 128:]
            c2, s2 = far_cos[k1:k1 + 1, own], far_sin[k1:k1 + 1, own]
            total_real = total_real + (c2 * u - s2 * v)
            total_imag = total_imag + (c2 * v + s2 * u)
        stacked += [total_real, total_imag]
    pages_ref[:, j, :] = jnp.transpose(jnp.concatenate(stacked, axis=0))


def vertical_table(vert_ref):
    fields, levels, _ = vert_ref.shape
    spread = (iota((2 * levels, levels), 0) // 2 == iota((2 * levels, levels), 1)).astype(F32)
    rows = jnp.concatenate(
        [lax.dot_general(spread, vert_ref[f], NT, precision=lax.Precision.HIGHEST,
                         preferred_element_type=F32) for f in range(fields)], axis=0)
    column = iota((levels, 512), 1)
    pick = (iota((levels, 512), 0) == 4 * (column // 128) + column % 4).astype(F32)
    block = jnp.dot(rows, pick, precision=lax.Precision.HIGHEST, preferred_element_type=F32)
    shape = block.shape
    row, column = iota(shape, 0), iota(shape, 1)
    keep = (row // (2 * levels) == column // 4 % 4) & (row % 2 == column // 16 % 2)
    block = jnp.where(keep, block, 0.0)
    slot = column // 32 % 4
    return jnp.concatenate([jnp.where(slot == i, block, 0.0) for i in range(4)], axis=0)


def finish(first_slot, order_ref, vert, pages_ref, joined_ref, table_ref, out_ref):
    levs, waves, rows, _ = pages_ref.shape
    for s in range(levs * waves):
        joined_ref[rows * s:rows * (s + 1), :] = pages_ref[s // waves, s % waves].astype(F32)
    high = vert.astype(BF16)
    low = (vert - high.astype(F32)).astype(BF16)
    mixed = None
    for v in range(4):
        block = joined_ref[128 * v:128 * (v + 1), :].astype(BF16)
        own = slice(128 * v, 128 * (v + 1))
        for part in (high, low):
            term = lax.dot_general(part[:, own], block, NT, preferred_element_type=F32)
            mixed = term if mixed is None else mixed + term
    mixed_high = mixed.astype(BF16)
    mixed_low = (mixed - mixed_high.astype(F32)).astype(BF16)
    both = jnp.concatenate([mixed_high, mixed_low], axis=1)
    fields, levels = out_ref.shape[0], out_ref.shape[1]
    lines = fields * levels * 2
    for i in range(4):
        table = jnp.concatenate([table_ref[v, i] for v in range(4)], axis=0)
        table = jnp.concatenate([table, table], axis=1)
        summed = lax.dot_general(both[lines * i:lines * (i + 1)], table, NT,
                                 preferred_element_type=F32)
        degree = iota(summed.shape, 1)
        summed = jnp.where(degree >= order_ref[first_slot + i], summed, 0.0)
        for q in range(fields * levels):
            out_ref[q // levels, q % levels, i] = summed[2 * q:2 * q + 2]


def kernel(waves, levs, grid_hbm, wind_hbm, points_hbm, order_hbm, orders_hbm, legendre_ref,
           vert_hbm, out_ref, grid_ref, wind_ref, points_ref, order_ref, orders_ref, vert_ref,
           rows_ref, pages_ref, send_ref, middle_ref, recv_ref, joined_ref, table_ref,
           fetch_sem, wave_send_sem, wave_recv_sem, lev_send_sem, lev_recv_sem, table_send_sem,
           table_recv_sem, local_sem):
    w, v = lax.axis_index("wave"), lax.axis_index("lev")
    me = w * levs + v
    fetches = [
        pltpu.make_async_copy(source, target, fetch_sem.at[at])
        for at, (source, target) in enumerate((
            (grid_hbm, grid_ref), (wind_hbm, wind_ref), (points_hbm, points_ref),
            (order_hbm, order_ref), (orders_hbm, orders_ref), (vert_hbm, vert_ref)))
    ]
    for fetch in fetches:
        fetch.start()
    own_table = pltpu.make_async_copy(
        legendre_ref.at[pl.ds(4 * v, 4)], table_ref.at[v], local_sem.at[0])
    own_table.start()

    barrier = pltpu.get_barrier_semaphore()
    for step in range(1, levs):
        pl.semaphore_signal(barrier, inc=1, device_id=(w, lax.rem(v + step, levs)),
                            device_id_type=MESH)

    def greet(step, carry):
        pl.semaphore_signal(barrier, inc=1, device_id=(lax.rem(w + step, waves), v),
                            device_id_type=MESH)
        return carry

    lax.fori_loop(1, waves, greet, 0)
    for fetch in fetches:
        fetch.wait()
    orders = column_orders(orders_ref)
    pl.semaphore_wait(barrier, waves - 1 + levs - 1)

    table_copies = []
    for step in (2, 1, 3):
        u = lax.rem(v + step, levs)
        copy = pltpu.make_async_remote_copy(
            src_ref=legendre_ref.at[pl.ds(4 * u, 4)], dst_ref=table_ref.at[v],
            send_sem=table_send_sem.at[step - 1], recv_sem=table_recv_sem.at[step - 1],
            device_id=(w, u), device_id_type=MESH)
        copy.start()
        table_copies.append(copy)

    advect(grid_ref, wind_ref, points_ref, rows_ref)
    for j in range(4):
        row_transform(j, points_ref, orders, rows_ref, pages_ref)
    send_ref[...] = pages_ref[...].astype(BF16).reshape(send_ref.shape)

    def send(step, carry):
        target = lax.rem(w + step, waves)
        pltpu.make_async_remote_copy(
            src_ref=send_ref.at[target], dst_ref=middle_ref.at[:, w], send_sem=wave_send_sem,
            recv_sem=wave_recv_sem, device_id=(target, v), device_id_type=MESH,
        ).start()
        return carry

    lax.fori_loop(1, waves, send, 0)
    own_pages = pltpu.make_async_copy(send_ref.at[w], middle_ref.at[:, w], local_sem.at[1])
    own_pages.start()
    vert = vertical_table(vert_ref)
    own_pages.wait()
    partner = {"device_id": (lax.rem(w + 1, waves), v), "device_id_type": MESH}
    arrived = middle_ref.at[:, pl.ds(0, waves - 1)]
    pltpu.make_async_remote_copy(
        src_ref=arrived, dst_ref=arrived, send_sem=wave_send_sem, recv_sem=wave_recv_sem,
        **partner).wait_recv()

    lev_copies = []
    for step in (2, 1, 3):
        u = lax.rem(v + step, levs)
        copy = pltpu.make_async_remote_copy(
            src_ref=middle_ref.at[u], dst_ref=recv_ref.at[v],
            send_sem=lev_send_sem.at[step - 1], recv_sem=lev_recv_sem.at[step - 1],
            device_id=(w, u), device_id_type=MESH)
        copy.start()
        lev_copies.append(copy)
    own_block = pltpu.make_async_copy(middle_ref.at[v], recv_ref.at[v], local_sem.at[2])
    own_block.start()
    left = send_ref.at[pl.ds(0, waves - 1)]
    pltpu.make_async_remote_copy(
        src_ref=left, dst_ref=left, send_sem=wave_send_sem, recv_sem=wave_recv_sem,
        **partner).wait_send()
    own_block.wait()
    own_table.wait()
    for copy in table_copies + lev_copies:
        copy.wait()
    finish(4 * me, order_ref, vert, recv_ref, joined_ref, table_ref, out_ref)


def body(grid_adjoint, courant, row_points, wave_order, legendre, vert_inverse, *, waves, levs):
    fields, levels, rows, width = grid_adjoint.shape
    slots = legendre.shape[0] // levs
    degrees = legendre.shape[1] * levs
    orders = wave_order.reshape(1, -1)
    hbm = pl.BlockSpec(memory_space=pltpu.HBM)
    return pl.pallas_call(
        functools.partial(kernel, waves, levs),
        out_shape=jax.ShapeDtypeStruct((fields, levels * levs, slots, 2, degrees), F32),
        in_specs=[hbm] * 7,
        out_specs=pl.BlockSpec(memory_space=pltpu.VMEM),
        scratch_shapes=[
            pltpu.VMEM(grid_adjoint.shape, BF16),
            pltpu.VMEM(courant.shape, BF16),
            pltpu.SMEM(row_points.shape, jnp.int32),
            pltpu.SMEM(wave_order.shape, jnp.int32),
            pltpu.VMEM(orders.shape, jnp.int32),
            pltpu.VMEM(vert_inverse.shape, F32),
            pltpu.VMEM((width // 128, 64, 128), F32),
            pltpu.VMEM((waves * levs, rows, 128), F32),
            pltpu.VMEM((waves, levs, rows, 128), BF16),
            pltpu.VMEM((levs, waves, rows, 128), BF16),
            pltpu.VMEM((levs, waves, rows, 128), BF16),
            pltpu.VMEM((levs * waves * rows, 128), F32),
            pltpu.VMEM((levs, slots) + legendre.shape[1:], BF16),
            pltpu.SemaphoreType.DMA((6,)),
            pltpu.SemaphoreType.DMA,
            pltpu.SemaphoreType.DMA,
            pltpu.SemaphoreType.DMA((levs - 1,)),
            pltpu.SemaphoreType.DMA((levs - 1,)),
            pltpu.SemaphoreType.DMA((levs - 1,)),
            pltpu.SemaphoreType.DMA((levs - 1,)),
            pltpu.SemaphoreType.DMA((3,)),
        ],
        compiler_params=pltpu.CompilerParams(
            collective_id=0, has_side_effects=True, vmem_limit_bytes=56 * 2**20),
    )(grid_adjoint, courant, row_points, wave_order, orders, legendre, vert_inverse)


def solution(mesh):
    return jax.shard_map(
        functools.partial(body, waves=mesh.shape["wave"], levs=mesh.shape["lev"]),
        mesh=mesh,
        in_specs=(
            P(None, "lev", "wave", None),
            P("lev", "wave", None),
            P("wave"),
            P(),
            P("wave", "lev", None),
            P(),
        ),
        out_specs=P(None, None, ("wave", "lev"), None, None),
        check_vma=False,
    )
```

```python
import functools

import jax
import jax.numpy as jnp
from jax import lax
from jax.experimental import pallas as pl
from jax.experimental.pallas import tpu as pltpu
from jax.sharding import PartitionSpec as P

F32 = jnp.float32
BF16 = jnp.bfloat16
MESH = pl.DeviceIdType.MESH
NT = (((1,), (1,)), ((), ()))

SIN_PI = (3.1415927410125732, -5.167712688446045, 2.5501632690429688,
          -0.5992521643638611, 0.08205024898052216, -0.007028118707239628)
COS_PI = (1.0, -4.934802055358887, 4.058709144592285,
          -1.3352118730545044, 0.2349366992712021, -0.024395223706960678)


def horner(coefficients, z):
    value = jnp.full(z.shape, coefficients[-1], F32)
    for c in coefficients[-2::-1]:
        value = value * z + c
    return value


def unit_circle(steps, orders, count):
    inverse = 1.0 / count
    product = steps * orders
    turns = jnp.floor(product * inverse + 0.5)
    x = (product - turns * count) * inverse
    z = x * x
    s = x * horner(SIN_PI, z)
    c = horner(COS_PI, z)
    return 1.0 - 2.0 * s * s, -2.0 * s * c


def iota(shape, axis):
    return lax.broadcasted_iota(jnp.int32, shape, axis)


def advect(grid_ref, wind_ref, points_ref, rows_ref):
    fields, levels, rows, width = grid_ref.shape
    shape = (2 * rows, width)
    row = iota(shape, 0) % rows
    count = jnp.full(shape, points_ref[0], jnp.int32)
    for j in range(1, rows):
        count = jnp.where(row == j, points_ref[j], count)
    position = iota(shape, 1)
    inside = position < count
    at_end = position == count - 1
    at_start = position == 0

    def pair(ref, *at):
        return jnp.concatenate(
            [ref[(*at[:-1], at[-1] + half)].astype(F32) for half in range(2)], axis=0)

    for level in range(0, levels, 2):
        wind = pair(wind_ref, level)
        for field in range(fields):
            grid = pair(grid_ref, field, level)
            flux = jnp.where(inside, wind * grid, 0.0)
            first = flux[:, :1]
            last = jnp.sum(jnp.where(at_end, flux, 0.0), axis=1, keepdims=True)
            forward = jnp.where(at_end, first, pltpu.roll(flux, width - 1, 1))
            backward = jnp.where(at_start, last, pltpu.roll(flux, 1, 1))
            result = jnp.where(inside, grid + 0.5 * (forward - backward), 0.0)
            at = rows * (field * levels + level)
            for k1 in range(width // 128):
                rows_ref[k1, at:at + 2 * rows, :] = result[:, 128 * k1:128 * (k1 + 1)]
    used = rows * fields * levels
    rows_ref[:, used:, :] = jnp.zeros((rows_ref.shape[0], rows_ref.shape[1] - used, 128), F32)


def column_orders(orders_ref):
    slots = orders_ref.shape[1]
    orders = orders_ref[...].astype(F32)
    high = jnp.floor(orders * 0.5)
    low = orders - 2.0 * high
    pick = (iota((slots, slots), 0) == 4 * (iota((slots, slots), 1) % 128)
            + iota((slots, slots), 1) // 128).astype(F32).astype(BF16)
    pair = jnp.concatenate([high, low, jnp.zeros((6, slots), F32)], axis=0).astype(BF16)
    moved = jnp.dot(pair, pick, preferred_element_type=F32)
    return 2.0 * moved[0:1] + moved[1:2]


def row_transform(j, points_ref, orders, rows_ref, pages_ref):
    blocks = rows_ref.shape[0]
    slots = orders.shape[1]
    count = jnp.full((1, slots), points_ref[j], jnp.int32).astype(F32)
    fine_cos, fine_sin = unit_circle(iota((16, 1), 0).astype(F32), orders, count)
    mid_cos, mid_sin = unit_circle(16.0 * iota((8, 1), 0).astype(F32), orders, count)
    far_cos, far_sin = unit_circle(128.0 * iota((16, 1), 0).astype(F32), orders, count)
    weight = jnp.where(2.0 * orders >= count, 0.0, jnp.where(orders == 0.0, 1.0, 2.0))
    far_cos = far_cos * weight
    far_sin = far_sin * weight
    left = jnp.concatenate(
        [rows_ref[k1, pl.ds(j, 16, stride=4), :] for k1 in range(blocks)], axis=0
    ).astype(BF16)
    stacked = []
    for i in range(slots // 128):
        own = slice(128 * i, 128 * (i + 1))
        c0, s0 = fine_cos[:, own], fine_sin[:, own]
        real, imag = [], []
        for b in range(8):
            c1, s1 = mid_cos[b:b + 1, own], mid_sin[b:b + 1, own]
            real.append(c1 * c0 - s1 * s0)
            imag.append(c1 * s0 + s1 * c0)
        table = jnp.concatenate(
            [jnp.concatenate(real, axis=0), jnp.concatenate(imag, axis=0)], axis=1
        ).astype(BF16)
        partial = jnp.dot(left, table, preferred_element_type=F32)
        total_real = jnp.zeros((16, 128), F32)
        total_imag = jnp.zeros((16, 128), F32)
        for k1 in range(blocks):
            u = partial[16 * k1:16 * (k1 + 1), :128]
            v = partial[16 * k1:16 * (k1 + 1), 128:]
            c2, s2 = far_cos[k1:k1 + 1, own], far_sin[k1:k1 + 1, own]
            total_real = total_real + (c2 * u - s2 * v)
            total_imag = total_imag + (c2 * v + s2 * u)
        stacked += [total_real, total_imag]
    pages_ref[:, j, :] = jnp.transpose(jnp.concatenate(stacked, axis=0))


def vertical_table(vert_ref):
    fields, levels, _ = vert_ref.shape
    spread = (iota((2 * levels, levels), 0) // 2 == iota((2 * levels, levels), 1)).astype(F32)
    rows = jnp.concatenate(
        [lax.dot_general(spread, vert_ref[f], NT, precision=lax.Precision.HIGHEST,
                         preferred_element_type=F32) for f in range(fields)], axis=0)
    column = iota((levels, 512), 1)
    pick = (iota((levels, 512), 0) == 4 * (column // 128) + column % 4).astype(F32)
    block = jnp.dot(rows, pick, precision=lax.Precision.HIGHEST, preferred_element_type=F32)
    shape = block.shape
    row, column = iota(shape, 0), iota(shape, 1)
    keep = (row // (2 * levels) == column // 4 % 4) & (row % 2 == column // 16 % 2)
    block = jnp.where(keep, block, 0.0)
    slot = column // 32 % 4
    return jnp.concatenate([jnp.where(slot == i, block, 0.0) for i in range(4)], axis=0)


def finish(first_slot, order_ref, vert, pages_ref, joined_ref, table_ref, out_ref):
    levs, waves, rows, _ = pages_ref.shape
    for s in range(levs * waves):
        joined_ref[rows * s:rows * (s + 1), :] = pages_ref[s // waves, s % waves].astype(F32)
    high = vert.astype(BF16)
    low = (vert - high.astype(F32)).astype(BF16)
    mixed = None
    for v in range(4):
        block = joined_ref[128 * v:128 * (v + 1), :].astype(BF16)
        own = slice(128 * v, 128 * (v + 1))
        for part in (high, low):
            term = lax.dot_general(part[:, own], block, NT, preferred_element_type=F32)
            mixed = term if mixed is None else mixed + term
    mixed_high = mixed.astype(BF16)
    mixed_low = (mixed - mixed_high.astype(F32)).astype(BF16)
    both = jnp.concatenate([mixed_high, mixed_low], axis=1)
    fields, levels = out_ref.shape[0], out_ref.shape[1]
    lines = fields * levels * 2
    for i in range(4):
        table = jnp.concatenate([table_ref[v, i] for v in range(4)], axis=0)
        table = jnp.concatenate([table, table], axis=1)
        summed = lax.dot_general(both[lines * i:lines * (i + 1)], table, NT,
                                 preferred_element_type=F32)
        degree = iota(summed.shape, 1)
        summed = jnp.where(degree >= order_ref[first_slot + i], summed, 0.0)
        for q in range(fields * levels):
            out_ref[q // levels, q % levels, i] = summed[2 * q:2 * q + 2]


def kernel(waves, levs, grid_hbm, wind_hbm, points_hbm, order_hbm, orders_hbm, legendre_ref,
           vert_hbm, out_ref, grid_ref, wind_ref, points_ref, order_ref, orders_ref, vert_ref,
           rows_ref, pages_ref, send_ref, middle_ref, recv_ref, joined_ref, table_ref,
           fetch_sem, wave_send_sem, wave_recv_sem, lev_send_sem, lev_recv_sem, table_send_sem,
           table_recv_sem, local_sem):
    w, v = lax.axis_index("wave"), lax.axis_index("lev")
    me = w * levs + v
    fetches = [
        pltpu.make_async_copy(source, target, fetch_sem.at[at])
        for at, (source, target) in enumerate((
            (grid_hbm, grid_ref), (wind_hbm, wind_ref), (points_hbm, points_ref),
            (order_hbm, order_ref), (orders_hbm, orders_ref), (vert_hbm, vert_ref)))
    ]
    for fetch in fetches:
        fetch.start()
    own_table = pltpu.make_async_copy(
        legendre_ref.at[pl.ds(4 * v, 4)], table_ref.at[v], local_sem.at[0])
    own_table.start()

    barrier = pltpu.get_barrier_semaphore()
    for step in range(1, levs):
        pl.semaphore_signal(barrier, inc=1, device_id=(w, lax.rem(v + step, levs)),
                            device_id_type=MESH)

    def greet(step, carry):
        pl.semaphore_signal(barrier, inc=1, device_id=(lax.rem(w + step, waves), v),
                            device_id_type=MESH)
        return carry

    lax.fori_loop(1, waves, greet, 0)
    for fetch in fetches:
        fetch.wait()
    orders = column_orders(orders_ref)
    pl.semaphore_wait(barrier, waves - 1 + levs - 1)

    table_copies = []
    for step in (2, 1, 3):
        u = lax.rem(v + step, levs)
        copy = pltpu.make_async_remote_copy(
            src_ref=legendre_ref.at[pl.ds(4 * u, 4)], dst_ref=table_ref.at[v],
            send_sem=table_send_sem.at[step - 1], recv_sem=table_recv_sem.at[step - 1],
            device_id=(w, u), device_id_type=MESH)
        copy.start()
        table_copies.append(copy)

    advect(grid_ref, wind_ref, points_ref, rows_ref)
    for j in range(4):
        row_transform(j, points_ref, orders, rows_ref, pages_ref)
    send_ref[...] = pages_ref[...].astype(BF16).reshape(send_ref.shape)

    def send(step, carry):
        target = lax.rem(w + step, waves)
        pltpu.make_async_remote_copy(
            src_ref=send_ref.at[target], dst_ref=middle_ref.at[:, w], send_sem=wave_send_sem,
            recv_sem=wave_recv_sem, device_id=(target, v), device_id_type=MESH,
        ).start()
        return carry

    lax.fori_loop(1, waves, send, 0)
    own_pages = pltpu.make_async_copy(send_ref.at[w], middle_ref.at[:, w], local_sem.at[1])
    own_pages.start()
    vert = vertical_table(vert_ref)
    own_pages.wait()
    partner = {"device_id": (lax.rem(w + 1, waves), v), "device_id_type": MESH}
    arrived = middle_ref.at[:, pl.ds(0, waves - 1)]
    pltpu.make_async_remote_copy(
        src_ref=arrived, dst_ref=arrived, send_sem=wave_send_sem, recv_sem=wave_recv_sem,
        **partner).wait_recv()

    lev_copies = []
    for step in (2, 1, 3):
        u = lax.rem(v + step, levs)
        copy = pltpu.make_async_remote_copy(
            src_ref=middle_ref.at[u], dst_ref=recv_ref.at[v],
            send_sem=lev_send_sem.at[step - 1], recv_sem=lev_recv_sem.at[step - 1],
            device_id=(w, u), device_id_type=MESH)
        copy.start()
        lev_copies.append(copy)
    own_block = pltpu.make_async_copy(middle_ref.at[v], recv_ref.at[v], local_sem.at[2])
    own_block.start()
    left = send_ref.at[pl.ds(0, waves - 1)]
    pltpu.make_async_remote_copy(
        src_ref=left, dst_ref=left, send_sem=wave_send_sem, recv_sem=wave_recv_sem,
        **partner).wait_send()
    own_block.wait()
    own_table.wait()
    for copy in table_copies + lev_copies:
        copy.wait()
    finish(4 * me, order_ref, vert, recv_ref, joined_ref, table_ref, out_ref)


def body(grid_adjoint, courant, row_points, wave_order, legendre, vert_inverse, *, waves, levs):
    fields, levels, rows, width = grid_adjoint.shape
    slots = legendre.shape[0] // levs
    degrees = legendre.shape[1] * levs
    orders = wave_order.reshape(1, -1)
    hbm = pl.BlockSpec(memory_space=pltpu.HBM)
    return pl.pallas_call(
        functools.partial(kernel, waves, levs),
        out_shape=pltpu.VMEM((fields, levels * levs, slots, 2, degrees), F32),
        in_specs=[hbm] * 7,
        out_specs=pl.BlockSpec(memory_space=pltpu.VMEM),
        scratch_shapes=[
            pltpu.VMEM(grid_adjoint.shape, BF16),
            pltpu.VMEM(courant.shape, BF16),
            pltpu.SMEM(row_points.shape, jnp.int32),
            pltpu.SMEM(wave_order.shape, jnp.int32),
            pltpu.VMEM(orders.shape, jnp.int32),
            pltpu.VMEM(vert_inverse.shape, F32),
            pltpu.VMEM((width // 128, 64, 128), F32),
            pltpu.VMEM((waves * levs, rows, 128), F32),
            pltpu.VMEM((waves, levs, rows, 128), BF16),
            pltpu.VMEM((levs, waves, rows, 128), BF16),
            pltpu.VMEM((levs, waves, rows, 128), BF16),
            pltpu.VMEM((levs * waves * rows, 128), F32),
            pltpu.VMEM((levs, slots) + legendre.shape[1:], BF16),
            pltpu.SemaphoreType.DMA((6,)),
            pltpu.SemaphoreType.DMA,
            pltpu.SemaphoreType.DMA,
            pltpu.SemaphoreType.DMA((levs - 1,)),
            pltpu.SemaphoreType.DMA((levs - 1,)),
            pltpu.SemaphoreType.DMA((levs - 1,)),
            pltpu.SemaphoreType.DMA((levs - 1,)),
            pltpu.SemaphoreType.DMA((3,)),
        ],
        compiler_params=pltpu.CompilerParams(
            collective_id=0, has_side_effects=True, vmem_limit_bytes=56 * 2**20),
    )(grid_adjoint, courant, row_points, wave_order, orders, legendre, vert_inverse)


def solution(mesh):
    return jax.shard_map(
        functools.partial(body, waves=mesh.shape["wave"], levs=mesh.shape["lev"]),
        mesh=mesh,
        in_specs=(
            P(None, "lev", "wave", None),
            P("lev", "wave", None),
            P("wave"),
            P(),
            P("wave", "lev", None),
            P(),
        ),
        out_specs=P(None, None, ("wave", "lev"), None, None),
        check_vma=False,
    )
```

```python
import functools

import jax
import jax.numpy as jnp
from jax import lax
from jax.experimental import pallas as pl
from jax.experimental.pallas import tpu as pltpu
from jax.sharding import PartitionSpec as P

F32 = jnp.float32
BF16 = jnp.bfloat16
MESH = pl.DeviceIdType.MESH
NT = (((1,), (1,)), ((), ()))

SIN_PI = (3.1415927410125732, -5.167712688446045, 2.5501632690429688,
          -0.5992521643638611, 0.08205024898052216, -0.007028118707239628)
COS_PI = (1.0, -4.934802055358887, 4.058709144592285,
          -1.3352118730545044, 0.2349366992712021, -0.024395223706960678)


def horner(coefficients, z):
    value = jnp.full(z.shape, coefficients[-1], F32)
    for c in coefficients[-2::-1]:
        value = value * z + c
    return value


def unit_circle(steps, orders, count):
    inverse = 1.0 / count
    product = steps * orders
    turns = jnp.floor(product * inverse + 0.5)
    x = (product - turns * count) * inverse
    z = x * x
    s = x * horner(SIN_PI, z)
    c = horner(COS_PI, z)
    return 1.0 - 2.0 * s * s, -2.0 * s * c


def iota(shape, axis):
    return lax.broadcasted_iota(jnp.int32, shape, axis)


def advect(grid_ref, wind_ref, points_ref, rows_ref):
    fields, levels, rows, width = grid_ref.shape
    shape = (2 * rows, width)
    row = iota(shape, 0) % rows
    count = jnp.full(shape, points_ref[0], jnp.int32)
    for j in range(1, rows):
        count = jnp.where(row == j, points_ref[j], count)
    position = iota(shape, 1)
    inside = position < count
    at_end = position == count - 1
    at_start = position == 0

    def pair(ref, *at):
        return jnp.concatenate(
            [ref[(*at[:-1], at[-1] + half)].astype(F32) for half in range(2)], axis=0)

    for level in range(0, levels, 2):
        wind = pair(wind_ref, level)
        for field in range(fields):
            grid = pair(grid_ref, field, level)
            flux = jnp.where(inside, wind * grid, 0.0)
            first = flux[:, :1]
            last = jnp.sum(jnp.where(at_end, flux, 0.0), axis=1, keepdims=True)
            forward = jnp.where(at_end, first, pltpu.roll(flux, width - 1, 1))
            backward = jnp.where(at_start, last, pltpu.roll(flux, 1, 1))
            result = jnp.where(inside, grid + 0.5 * (forward - backward), 0.0)
            at = rows * (field * levels + level)
            for k1 in range(width // 128):
                rows_ref[k1, at:at + 2 * rows, :] = result[:, 128 * k1:128 * (k1 + 1)]
    used = rows * fields * levels
    rows_ref[:, used:, :] = jnp.zeros((rows_ref.shape[0], rows_ref.shape[1] - used, 128), F32)


def column_orders(orders_ref):
    slots = orders_ref.shape[1]
    orders = orders_ref[...].astype(F32)
    high = jnp.floor(orders * 0.5)
    low = orders - 2.0 * high
    column = iota((slots, slots), 1)
    pick = (iota((slots, slots), 0) == 16 * (column % 32) + 4 * (column // 32 % 4)
            + column // 128).astype(F32).astype(BF16)
    pair = jnp.concatenate([high, low, jnp.zeros((6, slots), F32)], axis=0).astype(BF16)
    moved = jnp.dot(pair, pick, preferred_element_type=F32)
    return 2.0 * moved[0:1] + moved[1:2]


def row_tables(j, points_ref, orders, near_ref, far_ref):
    slots = orders.shape[1]
    count = jnp.full((1, slots), points_ref[j], jnp.int32).astype(F32)
    fine_cos, fine_sin = unit_circle(iota((16, 1), 0).astype(F32), orders, count)
    mid_cos, mid_sin = unit_circle(16.0 * iota((8, 1), 0).astype(F32), orders, count)
    far_cos, far_sin = unit_circle(128.0 * iota((16, 1), 0).astype(F32), orders, count)
    weight = jnp.where(2.0 * orders >= count, 0.0, jnp.where(orders == 0.0, 1.0, 2.0))
    far_ref[j, 0] = far_cos * weight
    far_ref[j, 1] = far_sin * weight
    for i in range(slots // 128):
        own = slice(128 * i, 128 * (i + 1))
        c0, s0 = fine_cos[:, own], fine_sin[:, own]
        real, imag = [], []
        for b in range(8):
            c1, s1 = mid_cos[b:b + 1, own], mid_sin[b:b + 1, own]
            real.append(c1 * c0 - s1 * s0)
            imag.append(c1 * s0 + s1 * c0)
        near_ref[j, i] = jnp.concatenate(
            [jnp.concatenate(real, axis=0), jnp.concatenate(imag, axis=0)], axis=1
        ).astype(BF16)


def row_transform(j, near_ref, far_ref, rows_ref, pages_ref):
    blocks = rows_ref.shape[0]
    left = jnp.concatenate(
        [rows_ref[k1, pl.ds(j, 16, stride=4), :] for k1 in range(blocks)], axis=0
    ).astype(BF16)
    stacked = []
    for i in range(near_ref.shape[1]):
        own = slice(128 * i, 128 * (i + 1))
        partial = jnp.dot(left, near_ref[j, i], preferred_element_type=F32)
        total_real = jnp.zeros((16, 128), F32)
        total_imag = jnp.zeros((16, 128), F32)
        for k1 in range(blocks):
            u = partial[16 * k1:16 * (k1 + 1), :128]
            v = partial[16 * k1:16 * (k1 + 1), 128:]
            c2, s2 = far_ref[j, 0, k1:k1 + 1, own], far_ref[j, 1, k1:k1 + 1, own]
            total_real = total_real + (c2 * u - s2 * v)
            total_imag = total_imag + (c2 * v + s2 * u)
        stacked += [total_real, total_imag]
    pages_ref[:, j, :] = jnp.transpose(jnp.concatenate(stacked, axis=0))


def vertical_table(vert_ref):
    fields, levels, _ = vert_ref.shape
    spread = (iota((2 * levels, levels), 0) // 2 == iota((2 * levels, levels), 1)).astype(F32)
    rows = jnp.concatenate(
        [lax.dot_general(spread, vert_ref[f], NT, precision=lax.Precision.HIGHEST,
                         preferred_element_type=F32) for f in range(fields)], axis=0)
    column = iota((levels, 512), 1)
    pick = (iota((levels, 512), 0) == 4 * (column // 128) + column % 4).astype(F32)
    block = jnp.dot(rows, pick, precision=lax.Precision.HIGHEST, preferred_element_type=F32)
    shape = block.shape
    row, column = iota(shape, 0), iota(shape, 1)
    keep = (row // (2 * levels) == column // 4 % 4) & (row % 2 == column // 16 % 2)
    block = jnp.where(keep, block, 0.0)
    slot = column // 32 % 4
    return jnp.concatenate([jnp.where(slot == i, block, 0.0) for i in range(4)], axis=0)


def finish(first_slot, order_ref, vert, pages_ref, joined_ref, table_ref, out_ref):
    levs, waves, rows, _ = pages_ref.shape
    for s in range(levs * waves):
        joined_ref[rows * s:rows * (s + 1), :] = pages_ref[s // waves, s % waves].astype(F32)
    high = vert.astype(BF16)
    low = (vert - high.astype(F32)).astype(BF16)
    mixed = None
    for v in range(4):
        block = joined_ref[128 * v:128 * (v + 1), :].astype(BF16)
        own = slice(128 * v, 128 * (v + 1))
        for part in (high, low):
            term = lax.dot_general(part[:, own], block, NT, preferred_element_type=F32)
            mixed = term if mixed is None else mixed + term
    mixed_high = mixed.astype(BF16)
    mixed_low = (mixed - mixed_high.astype(F32)).astype(BF16)
    both = jnp.concatenate([mixed_high, mixed_low], axis=1)
    fields, levels = out_ref.shape[0], out_ref.shape[1]
    lines = fields * levels * 2
    for i in range(4):
        table = jnp.concatenate([table_ref[v, i] for v in range(4)], axis=0)
        table = jnp.concatenate([table, table], axis=1)
        summed = lax.dot_general(both[lines * i:lines * (i + 1)], table, NT,
                                 preferred_element_type=F32)
        degree = iota(summed.shape, 1)
        summed = jnp.where(degree >= order_ref[first_slot + i], summed, 0.0)
        for q in range(fields * levels):
            out_ref[q // levels, q % levels, i] = summed[2 * q:2 * q + 2]


def kernel(waves, levs, grid_hbm, wind_hbm, points_hbm, order_hbm, orders_hbm, legendre_ref,
           vert_hbm, out_ref, grid_ref, wind_ref, points_ref, order_ref, orders_ref, vert_ref,
           near_ref, far_ref, rows_ref, pages_ref, send_ref, middle_ref, recv_ref, joined_ref, table_ref,
           fetch_sem, wave_send_sem, wave_recv_sem, lev_send_sem, lev_recv_sem, table_send_sem,
           table_recv_sem, local_sem, near_sem):
    w, v = lax.axis_index("wave"), lax.axis_index("lev")
    me = w * levs + v
    fetches = [
        pltpu.make_async_copy(source, target, fetch_sem.at[at])
        for at, (source, target) in enumerate((
            (grid_hbm, grid_ref), (wind_hbm, wind_ref), (points_hbm, points_ref),
            (order_hbm, order_ref), (orders_hbm, orders_ref), (vert_hbm, vert_ref)))
    ]
    for fetch in fetches:
        fetch.start()
    own_table = pltpu.make_async_copy(
        legendre_ref.at[pl.ds(4 * v, 4)], table_ref.at[v], local_sem.at[5])
    own_table.start()

    planes, places = waves // 8, 8
    plane, place = w // places, lax.rem(w, places)
    mate = w + 1 - 2 * lax.rem(w, 2)
    along_y = [places * plane + lax.rem(place + 2 * step, places) for step in range(1, 4)]

    def others(first, last, action):
        def one(step, carry):
            target_plane = first + step // 6
            target = places * target_plane + lax.rem(
                2 * (place // 2) + 2 + lax.rem(step, 6), places)
            action(target, target_plane)
            return carry

        lax.fori_loop(0, 6 * (last - first), one, 0)

    barrier = pltpu.get_barrier_semaphore()

    def greet(target, lev):
        pl.semaphore_signal(barrier, inc=1, device_id=(target, lev), device_id_type=MESH)

    for step in range(1, levs):
        greet(w, lax.rem(v + step, levs))
    for step in range(planes):
        greet(lax.rem(mate + places * step, waves), v)
        if step > 0:
            greet(lax.rem(w + places * step, waves), v)
    others(plane, plane + 1, lambda target, _: greet(target, v))
    others(plane + 1, planes, lambda target, _: greet(target, v))
    for fetch in fetches[2:5]:
        fetch.wait()
    orders = column_orders(orders_ref)
    for j in range(4):
        row_tables(j, points_ref, orders, near_ref, far_ref)
    fetches[0].wait()
    fetches[1].wait()
    advect(grid_ref, wind_ref, points_ref, rows_ref)
    for j in range(4):
        row_transform(j, near_ref, far_ref, rows_ref, pages_ref)
    send_ref[...] = pages_ref[...].astype(BF16).reshape(send_ref.shape)
    table_copies = []

    def send_table(step, first, count):
        u = lax.rem(v + step, levs)
        at = len(table_copies)
        copy = pltpu.make_async_remote_copy(
            src_ref=legendre_ref.at[pl.ds(4 * u + first, count)],
            dst_ref=table_ref.at[v, pl.ds(first, count)],
            send_sem=table_send_sem.at[at], recv_sem=table_recv_sem.at[at],
            device_id=(w, u), device_id_type=MESH)
        copy.start()
        table_copies.append(copy)

    own_pages = pltpu.make_async_copy(send_ref.at[:, w], middle_ref.at[:, w], local_sem.at[4])
    own_pages.start()
    pl.semaphore_wait(barrier, levs - 1 + 2 * planes - 1 + 6 + 6 * plane)
    for target in along_y:
        pl.semaphore_signal(near_sem, inc=1, device_id=(target, v), device_id_type=MESH)

    def send(target, target_plane):
        turn = lax.rem(target_plane + planes - plane, planes)
        pltpu.make_async_remote_copy(
            src_ref=send_ref.at[:, target], dst_ref=middle_ref.at[:, w],
            send_sem=wave_send_sem, recv_sem=wave_recv_sem.at[turn],
            device_id=(target, v), device_id_type=MESH,
        ).start()

    others(0, plane, send)
    for step in (2, 1, 3, 0):
        target_plane = lax.rem(plane + step, planes)
        send(lax.rem(mate + places * step, waves), target_plane)
        if step > 0:
            send(lax.rem(w + places * step, waves), target_plane)
    others(plane, plane + 1, send)
    send_table(1, 0, 4)
    send_table(3, 0, 4)
    pl.semaphore_wait(near_sem, len(along_y))
    others(plane + 1, planes, send)
    send_table(2, 0, 4)
    fetches[5].wait()
    vert = vertical_table(vert_ref)
    own_pages.wait()
    partner = {"device_id": (mate, v), "device_id_type": MESH}
    lev_copies, own_blocks = [], []
    for turn in (0, 1, 3, 2):
        arrived = middle_ref.at[:, pl.ds(0, 7 if turn == 0 else 8)]
        pltpu.make_async_remote_copy(
            src_ref=arrived, dst_ref=arrived, send_sem=wave_send_sem,
            recv_sem=wave_recv_sem.at[turn], **partner).wait_recv()
        part = pl.ds(8 * lax.rem(plane + 4 - turn, 4), 8)
        for step in (2, 1, 3):
            u = lax.rem(v + step, levs)
            at = 3 * turn + step - 1
            copy = pltpu.make_async_remote_copy(
                src_ref=middle_ref.at[u, part], dst_ref=recv_ref.at[v, part],
                send_sem=lev_send_sem.at[at], recv_sem=lev_recv_sem.at[at],
                device_id=(w, u), device_id_type=MESH)
            copy.start()
            lev_copies.append(copy)
        copy = pltpu.make_async_copy(
            middle_ref.at[v, part], recv_ref.at[v, part], local_sem.at[turn])
        copy.start()
        own_blocks.append(copy)
    own_table.wait()
    for copy in own_blocks + table_copies + lev_copies:
        copy.wait()
    finish(4 * me, order_ref, vert, recv_ref, joined_ref, table_ref, out_ref)
    left = send_ref.at[:, pl.ds(0, waves - 1)]
    pltpu.make_async_remote_copy(
        src_ref=left, dst_ref=left, send_sem=wave_send_sem, recv_sem=wave_recv_sem.at[0],
        **partner).wait_send()


def body(grid_adjoint, courant, row_points, wave_order, legendre, vert_inverse, *, waves, levs):
    fields, levels, rows, width = grid_adjoint.shape
    slots = legendre.shape[0] // levs
    degrees = legendre.shape[1] * levs
    orders = wave_order.reshape(1, -1)
    hbm = pl.BlockSpec(memory_space=pltpu.HBM)
    return pl.pallas_call(
        functools.partial(kernel, waves, levs),
        out_shape=pltpu.VMEM((fields, levels * levs, slots, 2, degrees), F32),
        in_specs=[hbm] * 7,
        out_specs=pl.BlockSpec(memory_space=pltpu.VMEM),
        scratch_shapes=[
            pltpu.VMEM(grid_adjoint.shape, BF16),
            pltpu.VMEM(courant.shape, BF16),
            pltpu.SMEM(row_points.shape, jnp.int32),
            pltpu.SMEM(wave_order.shape, jnp.int32),
            pltpu.VMEM(orders.shape, jnp.int32),
            pltpu.VMEM(vert_inverse.shape, F32),
            pltpu.VMEM((rows, 4, 128, 256), BF16),
            pltpu.VMEM((rows, 2, 16, 512), F32),
            pltpu.VMEM((width // 128, 64, 128), F32),
            pltpu.VMEM((waves * levs, rows, 128), F32),
            pltpu.VMEM((levs, waves, rows, 128), BF16),
            pltpu.VMEM((levs, waves, rows, 128), BF16),
            pltpu.VMEM((levs, waves, rows, 128), BF16),
            pltpu.VMEM((levs * waves * rows, 128), F32),
            pltpu.VMEM((levs, slots) + legendre.shape[1:], BF16),
            pltpu.SemaphoreType.DMA((6,)),
            pltpu.SemaphoreType.DMA,
            pltpu.SemaphoreType.DMA((4,)),
            pltpu.SemaphoreType.DMA((12,)),
            pltpu.SemaphoreType.DMA((12,)),
            pltpu.SemaphoreType.DMA((8,)),
            pltpu.SemaphoreType.DMA((8,)),
            pltpu.SemaphoreType.DMA((6,)),
            pltpu.SemaphoreType.REGULAR,
        ],
        compiler_params=pltpu.CompilerParams(
            collective_id=0, has_side_effects=True, vmem_limit_bytes=56 * 2**20),
    )(grid_adjoint, courant, row_points, wave_order, orders, legendre, vert_inverse)


def solution(mesh):
    return jax.shard_map(
        functools.partial(body, waves=mesh.shape["wave"], levs=mesh.shape["lev"]),
        mesh=mesh,
        in_specs=(
            P(None, "lev", "wave", None),
            P("lev", "wave", None),
            P("wave"),
            P(),
            P("wave", "lev", None),
            P(),
        ),
        out_specs=P(None, None, ("wave", "lev"), None, None),
        check_vma=False,
    )
```

```python
import functools

import jax
import jax.numpy as jnp
from jax import lax
from jax.experimental import pallas as pl
from jax.experimental.pallas import tpu as pltpu
from jax.sharding import PartitionSpec as P

F32 = jnp.float32
BF16 = jnp.bfloat16
MESH = pl.DeviceIdType.MESH
NT = (((1,), (1,)), ((), ()))

SIN_PI = (3.1415927410125732, -5.167712688446045, 2.5501632690429688,
          -0.5992521643638611, 0.08205024898052216, -0.007028118707239628)
COS_PI = (1.0, -4.934802055358887, 4.058709144592285,
          -1.3352118730545044, 0.2349366992712021, -0.024395223706960678)


def horner(coefficients, z):
    value = jnp.full(z.shape, coefficients[-1], F32)
    for c in coefficients[-2::-1]:
        value = value * z + c
    return value


def unit_circle(steps, orders, count):
    inverse = 1.0 / count
    product = steps * orders
    turns = jnp.floor(product * inverse + 0.5)
    x = (product - turns * count) * inverse
    z = x * x
    s = x * horner(SIN_PI, z)
    c = horner(COS_PI, z)
    return 1.0 - 2.0 * s * s, -2.0 * s * c


def iota(shape, axis):
    return lax.broadcasted_iota(jnp.int32, shape, axis)


def advect(grid_ref, wind_ref, points_ref, rows_ref):
    fields, levels, rows, width = grid_ref.shape
    shape = (2 * rows, width)
    row = iota(shape, 0) % rows
    count = jnp.full(shape, points_ref[0], jnp.int32)
    for j in range(1, rows):
        count = jnp.where(row == j, points_ref[j], count)
    position = iota(shape, 1)
    inside = position < count
    at_end = position == count - 1
    at_start = position == 0

    def pair(ref, *at):
        return jnp.concatenate(
            [ref[(*at[:-1], at[-1] + half)].astype(F32) for half in range(2)], axis=0)

    for level in range(0, levels, 2):
        wind = pair(wind_ref, level)
        for field in range(fields):
            grid = pair(grid_ref, field, level)
            flux = jnp.where(inside, wind * grid, 0.0)
            first = flux[:, :1]
            last = jnp.sum(jnp.where(at_end, flux, 0.0), axis=1, keepdims=True)
            forward = jnp.where(at_end, first, pltpu.roll(flux, width - 1, 1))
            backward = jnp.where(at_start, last, pltpu.roll(flux, 1, 1))
            result = jnp.where(inside, grid + 0.5 * (forward - backward), 0.0)
            at = rows * (field * levels + level)
            for k1 in range(width // 128):
                rows_ref[k1, at:at + 2 * rows, :] = result[:, 128 * k1:128 * (k1 + 1)]
    used = rows * fields * levels
    rows_ref[:, used:, :] = jnp.zeros((rows_ref.shape[0], rows_ref.shape[1] - used, 128), F32)


def column_orders(orders_ref, pick_ref):
    slots = orders_ref.shape[1]
    orders = orders_ref[...].astype(F32)
    high = jnp.floor(orders * 0.5)
    low = orders - 2.0 * high
    pair = jnp.concatenate([high, low, jnp.zeros((6, slots), F32)], axis=0).astype(BF16)
    moved = jnp.dot(pair, pick_ref[...], preferred_element_type=F32)
    return 2.0 * moved[0:1] + moved[1:2]


def row_tables(j, points_ref, orders, near_ref, far_ref):
    slots = orders.shape[1]
    count = jnp.full((1, slots), points_ref[j], jnp.int32).astype(F32)
    fine_cos, fine_sin = unit_circle(iota((16, 1), 0).astype(F32), orders, count)
    mid_cos, mid_sin = unit_circle(16.0 * iota((8, 1), 0).astype(F32), orders, count)
    far_cos, far_sin = unit_circle(128.0 * iota((16, 1), 0).astype(F32), orders, count)
    weight = jnp.where(2.0 * orders >= count, 0.0, jnp.where(orders == 0.0, 1.0, 2.0))
    far_ref[j, 0] = far_cos * weight
    far_ref[j, 1] = far_sin * weight
    for i in range(slots // 128):
        own = slice(128 * i, 128 * (i + 1))
        c0, s0 = fine_cos[:, own], fine_sin[:, own]
        real, imag = [], []
        for b in range(8):
            c1, s1 = mid_cos[b:b + 1, own], mid_sin[b:b + 1, own]
            real.append(c1 * c0 - s1 * s0)
            imag.append(c1 * s0 + s1 * c0)
        near_ref[j, i] = jnp.concatenate(
            [jnp.concatenate(real, axis=0), jnp.concatenate(imag, axis=0)], axis=1
        ).astype(BF16)


def row_transform(j, near_ref, far_ref, rows_ref, pages_ref):
    blocks = rows_ref.shape[0]
    left = jnp.concatenate(
        [rows_ref[k1, pl.ds(j, 16, stride=4), :] for k1 in range(blocks)], axis=0
    ).astype(BF16)
    stacked = []
    for i in range(near_ref.shape[1]):
        own = slice(128 * i, 128 * (i + 1))
        partial = jnp.dot(left, near_ref[j, i], preferred_element_type=F32)
        total_real = jnp.zeros((16, 128), F32)
        total_imag = jnp.zeros((16, 128), F32)
        for k1 in range(blocks):
            u = partial[16 * k1:16 * (k1 + 1), :128]
            v = partial[16 * k1:16 * (k1 + 1), 128:]
            c2, s2 = far_ref[j, 0, k1:k1 + 1, own], far_ref[j, 1, k1:k1 + 1, own]
            total_real = total_real + (c2 * u - s2 * v)
            total_imag = total_imag + (c2 * v + s2 * u)
        stacked += [total_real, total_imag]
    pages_ref[:, j, :] = jnp.transpose(jnp.concatenate(stacked, axis=0))


def vertical_table(vert_ref):
    fields, levels, _ = vert_ref.shape
    spread = (iota((2 * levels, levels), 0) // 2 == iota((2 * levels, levels), 1)).astype(F32)
    rows = jnp.concatenate(
        [lax.dot_general(spread, vert_ref[f], NT, precision=lax.Precision.HIGHEST,
                         preferred_element_type=F32) for f in range(fields)], axis=0)
    column = iota((levels, 512), 1)
    pick = (iota((levels, 512), 0) == 4 * (column // 128) + column % 4).astype(F32)
    block = jnp.dot(rows, pick, precision=lax.Precision.HIGHEST, preferred_element_type=F32)
    shape = block.shape
    row, column = iota(shape, 0), iota(shape, 1)
    keep = (row // (2 * levels) == column // 4 % 4) & (row % 2 == column // 16 % 2)
    block = jnp.where(keep, block, 0.0)
    slot = column // 32 % 4
    return jnp.concatenate([jnp.where(slot == i, block, 0.0) for i in range(4)], axis=0)


def finish(first_slot, order_ref, vert, joined_ref, table_ref, out_ref):
    high = vert.astype(BF16)
    low = (vert - high.astype(F32)).astype(BF16)
    mixed = None
    for v in range(4):
        block = joined_ref[128 * v:128 * (v + 1), :].astype(BF16)
        own = slice(128 * v, 128 * (v + 1))
        term = lax.dot_general(
            jnp.concatenate([high[:, own], low[:, own]], axis=1),
            jnp.concatenate([block, block], axis=1), NT, preferred_element_type=F32)
        mixed = term if mixed is None else mixed + term
    mixed_high = mixed.astype(BF16)
    mixed_low = (mixed - mixed_high.astype(F32)).astype(BF16)
    both = jnp.concatenate([mixed_high, mixed_low], axis=1)
    fields, levels = out_ref.shape[0], out_ref.shape[1]
    lines = fields * levels * 2
    for i in range(4):
        table = jnp.concatenate([table_ref[v, i] for v in range(4)], axis=0)
        table = jnp.concatenate([table, table], axis=1)
        summed = lax.dot_general(both[lines * i:lines * (i + 1)], table, NT,
                                 preferred_element_type=F32)
        degree = iota(summed.shape, 1)
        summed = jnp.where(degree >= order_ref[first_slot + i], summed, 0.0)
        for q in range(fields * levels):
            out_ref[q // levels, q % levels, i] = summed[2 * q:2 * q + 2]


def kernel(waves, levs, grid_hbm, wind_hbm, points_hbm, order_hbm, orders_hbm, legendre_ref,
           vert_hbm, out_ref, grid_ref, wind_ref, points_ref, order_ref, orders_ref, vert_ref,
           pick_ref, near_ref, far_ref, rows_ref, pages_ref, send_ref, middle_ref, recv_ref,
           joined_ref, table_ref,
           fetch_sem, wave_send_sem, wave_recv_sem, lev_send_sem, lev_recv_sem, table_send_sem,
           table_recv_sem, local_sem, near_sem):
    w, v = lax.axis_index("wave"), lax.axis_index("lev")
    me = w * levs + v
    fetches = [
        pltpu.make_async_copy(source, target, fetch_sem.at[at])
        for at, (source, target) in enumerate((
            (orders_hbm, orders_ref), (points_hbm, points_ref), (wind_hbm, wind_ref),
            (grid_hbm, grid_ref), (order_hbm, order_ref), (vert_hbm, vert_ref)))
    ]
    for fetch in fetches:
        fetch.start()
    own_table = pltpu.make_async_copy(
        legendre_ref.at[pl.ds(4 * v, 4)], table_ref.at[v], local_sem.at[5])
    own_table.start()

    planes, places = waves // 8, 8
    plane, place = w // places, lax.rem(w, places)
    mate = w + 1 - 2 * lax.rem(w, 2)
    along_y = [places * plane + lax.rem(place + 2 * step, places) for step in range(1, 4)]

    def others(first, last, action):
        def one(step, carry):
            target_plane = first + step // 6
            target = places * target_plane + lax.rem(
                2 * (place // 2) + 2 + lax.rem(step, 6), places)
            action(target, target_plane)
            return carry

        lax.fori_loop(0, 6 * (last - first), one, 0)

    barrier = pltpu.get_barrier_semaphore()

    def greet(target, lev):
        pl.semaphore_signal(barrier, inc=1, device_id=(target, lev), device_id_type=MESH)

    for step in range(1, levs):
        greet(w, lax.rem(v + step, levs))
    for step in range(planes):
        greet(lax.rem(mate + places * step, waves), v)
        if step > 0:
            greet(lax.rem(w + places * step, waves), v)
    others(plane, plane + 1, lambda target, _: greet(target, v))
    others(plane + 1, planes, lambda target, _: greet(target, v))
    order_count = orders_ref.shape[1]
    column = iota((order_count, order_count), 1)
    pick_ref[...] = (iota((order_count, order_count), 0) == 16 * (column % 32) + 4 * (column // 32 % 4)
            + column // 128).astype(F32).astype(BF16)
    fetches[0].wait()
    fetches[1].wait()
    orders = column_orders(orders_ref, pick_ref)
    for j in range(4):
        row_tables(j, points_ref, orders, near_ref, far_ref)
    fetches[2].wait()
    fetches[3].wait()
    advect(grid_ref, wind_ref, points_ref, rows_ref)
    for j in range(4):
        row_transform(j, near_ref, far_ref, rows_ref, pages_ref)
    send_ref[...] = pages_ref[...].astype(BF16).reshape(send_ref.shape)
    table_copies = []

    def send_table(step, first, count):
        u = lax.rem(v + step, levs)
        at = len(table_copies)
        copy = pltpu.make_async_remote_copy(
            src_ref=legendre_ref.at[pl.ds(4 * u + first, count)],
            dst_ref=table_ref.at[v, pl.ds(first, count)],
            send_sem=table_send_sem.at[at], recv_sem=table_recv_sem.at[at],
            device_id=(w, u), device_id_type=MESH)
        copy.start()
        table_copies.append(copy)

    own_pages = pltpu.make_async_copy(send_ref.at[:, w], middle_ref.at[:, w], wave_recv_sem.at[0])
    own_pages.start()
    pl.semaphore_wait(barrier, levs - 1 + 2 * planes - 1 + 6 + 6 * plane)
    for target in along_y:
        pl.semaphore_signal(near_sem, inc=1, device_id=(target, v), device_id_type=MESH)

    def send(target, target_plane):
        turn = lax.rem(target_plane + planes - plane, planes)
        pltpu.make_async_remote_copy(
            src_ref=send_ref.at[:, target], dst_ref=middle_ref.at[:, w],
            send_sem=wave_send_sem, recv_sem=wave_recv_sem.at[turn],
            device_id=(target, v), device_id_type=MESH,
        ).start()

    others(0, plane, send)
    for step in (2, 1, 3, 0):
        target_plane = lax.rem(plane + step, planes)
        send(lax.rem(mate + places * step, waves), target_plane)
        if step > 0:
            send(lax.rem(w + places * step, waves), target_plane)
    others(plane, plane + 1, send)
    send_table(1, 0, 4)
    send_table(3, 0, 4)
    pl.semaphore_wait(near_sem, len(along_y))
    others(plane + 1, planes, send)
    send_table(2, 0, 4)
    fetches[4].wait()
    fetches[5].wait()
    vert = vertical_table(vert_ref)
    partner = {"device_id": (mate, v), "device_id_type": MESH}
    lev_copies, own_blocks = [], []
    arrived = middle_ref.at[:, pl.ds(0, places)]
    for source in range(planes):
        turn = lax.rem(plane + planes - source, planes)
        pltpu.make_async_remote_copy(
            src_ref=arrived, dst_ref=arrived, send_sem=wave_send_sem,
            recv_sem=wave_recv_sem.at[turn], **partner).wait_recv()
        part = pl.ds(places * source, places)
        for step in (2, 1, 3):
            u = lax.rem(v + step, levs)
            at = 3 * source + step - 1
            copy = pltpu.make_async_remote_copy(
                src_ref=middle_ref.at[u, part], dst_ref=recv_ref.at[v, part],
                send_sem=lev_send_sem.at[at], recv_sem=lev_recv_sem.at[at],
                device_id=(w, u), device_id_type=MESH)
            copy.start()
            lev_copies.append(copy)
        copy = pltpu.make_async_copy(
            middle_ref.at[v, part], recv_ref.at[v, part], local_sem.at[source])
        copy.start()
        own_blocks.append(copy)
    own_table.wait()
    for copy in table_copies:
        copy.wait_recv()
    for source in range(planes):
        for copy in lev_copies[3 * source:3 * source + 3]:
            copy.wait_recv()
        own_blocks[source].wait()
        for lev in range(levs):
            for at in range(places):
                row = 4 * (waves * lev + places * source + at)
                joined_ref[row:row + 4, :] = recv_ref[lev, places * source + at].astype(F32)
    finish(4 * me, order_ref, vert, joined_ref, table_ref, out_ref)
    for copy in table_copies + lev_copies:
        copy.wait_send()
    left = send_ref.at[:, pl.ds(0, waves - 1)]
    pltpu.make_async_remote_copy(
        src_ref=left, dst_ref=left, send_sem=wave_send_sem, recv_sem=wave_recv_sem.at[0],
        **partner).wait_send()


def body(grid_adjoint, courant, row_points, wave_order, legendre, vert_inverse, *, waves, levs):
    fields, levels, rows, width = grid_adjoint.shape
    slots = legendre.shape[0] // levs
    degrees = legendre.shape[1] * levs
    orders = wave_order.reshape(1, -1)
    hbm = pl.BlockSpec(memory_space=pltpu.HBM)
    return pl.pallas_call(
        functools.partial(kernel, waves, levs),
        out_shape=pltpu.VMEM((fields, levels * levs, slots, 2, degrees), F32),
        in_specs=[hbm] * 7,
        out_specs=pl.BlockSpec(memory_space=pltpu.VMEM),
        scratch_shapes=[
            pltpu.VMEM(grid_adjoint.shape, BF16),
            pltpu.VMEM(courant.shape, BF16),
            pltpu.SMEM(row_points.shape, jnp.int32),
            pltpu.SMEM(wave_order.shape, jnp.int32),
            pltpu.VMEM(orders.shape, jnp.int32),
            pltpu.VMEM(vert_inverse.shape, F32),
            pltpu.VMEM((512, 512), BF16),
            pltpu.VMEM((rows, 4, 128, 256), BF16),
            pltpu.VMEM((rows, 2, 16, 512), F32),
            pltpu.VMEM((width // 128, 64, 128), F32),
            pltpu.VMEM((waves * levs, rows, 128), F32),
            pltpu.VMEM((levs, waves, rows, 128), BF16),
            pltpu.VMEM((levs, waves, rows, 128), BF16),
            pltpu.VMEM((levs, waves, rows, 128), BF16),
            pltpu.VMEM((levs * waves * rows, 128), F32),
            pltpu.VMEM((levs, slots) + legendre.shape[1:], BF16),
            pltpu.SemaphoreType.DMA((6,)),
            pltpu.SemaphoreType.DMA,
            pltpu.SemaphoreType.DMA((4,)),
            pltpu.SemaphoreType.DMA((12,)),
            pltpu.SemaphoreType.DMA((12,)),
            pltpu.SemaphoreType.DMA((8,)),
            pltpu.SemaphoreType.DMA((8,)),
            pltpu.SemaphoreType.DMA((6,)),
            pltpu.SemaphoreType.REGULAR,
        ],
        compiler_params=pltpu.CompilerParams(
            collective_id=0, has_side_effects=True, vmem_limit_bytes=56 * 2**20),
    )(grid_adjoint, courant, row_points, wave_order, orders, legendre, vert_inverse)


def solution(mesh):
    return jax.shard_map(
        functools.partial(body, waves=mesh.shape["wave"], levs=mesh.shape["lev"]),
        mesh=mesh,
        in_specs=(
            P(None, "lev", "wave", None),
            P("lev", "wave", None),
            P("wave"),
            P(),
            P("wave", "lev", None),
            P(),
        ),
        out_specs=P(None, None, ("wave", "lev"), None, None),
        check_vma=False,
    )
```

```python
import functools

import jax
import jax.numpy as jnp
from jax import lax
from jax.experimental import pallas as pl
from jax.experimental.pallas import tpu as pltpu
from jax.sharding import PartitionSpec as P

F32 = jnp.float32
BF16 = jnp.bfloat16
MESH = pl.DeviceIdType.MESH
NT = (((1,), (1,)), ((), ()))

SIN_PI = (3.1415927410125732, -5.167712688446045, 2.5501632690429688,
          -0.5992521643638611, 0.08205024898052216, -0.007028118707239628)
COS_PI = (1.0, -4.934802055358887, 4.058709144592285,
          -1.3352118730545044, 0.2349366992712021, -0.024395223706960678)


def horner(coefficients, z):
    value = jnp.full(z.shape, coefficients[-1], F32)
    for c in coefficients[-2::-1]:
        value = value * z + c
    return value


def unit_circle(steps, orders, count):
    inverse = 1.0 / count
    product = steps * orders
    turns = jnp.floor(product * inverse + 0.5)
    x = (product - turns * count) * inverse
    z = x * x
    s = x * horner(SIN_PI, z)
    c = horner(COS_PI, z)
    return 1.0 - 2.0 * s * s, -2.0 * s * c


def iota(shape, axis):
    return lax.broadcasted_iota(jnp.int32, shape, axis)


def advect(grid_ref, wind_ref, points_ref, rows_ref):
    fields, levels, rows, width = grid_ref.shape
    shape = (2 * rows, width)
    row = iota(shape, 0) % rows
    count = jnp.full(shape, points_ref[0], jnp.int32)
    for j in range(1, rows):
        count = jnp.where(row == j, points_ref[j], count)
    position = iota(shape, 1)
    inside = position < count
    at_end = position == count - 1
    at_start = position == 0

    def pair(ref, *at):
        return jnp.concatenate(
            [ref[(*at[:-1], at[-1] + half)].astype(F32) for half in range(2)], axis=0)

    for level in range(0, levels, 2):
        wind = pair(wind_ref, level)
        for field in range(fields):
            grid = pair(grid_ref, field, level)
            flux = jnp.where(inside, wind * grid, 0.0)
            first = flux[:, :1]
            last = jnp.sum(jnp.where(at_end, flux, 0.0), axis=1, keepdims=True)
            forward = jnp.where(at_end, first, pltpu.roll(flux, width - 1, 1))
            backward = jnp.where(at_start, last, pltpu.roll(flux, 1, 1))
            result = jnp.where(inside, grid + 0.5 * (forward - backward), 0.0)
            at = rows * (field * levels + level)
            for k1 in range(width // 128):
                rows_ref[k1, at:at + 2 * rows, :] = result[:, 128 * k1:128 * (k1 + 1)]
    used = rows * fields * levels
    rows_ref[:, used:, :] = jnp.zeros((rows_ref.shape[0], rows_ref.shape[1] - used, 128), F32)


def column_orders(orders_ref, pick_ref):
    slots = orders_ref.shape[1]
    orders = orders_ref[...].astype(F32)
    high = jnp.floor(orders * 0.5)
    low = orders - 2.0 * high
    pair = jnp.concatenate([high, low, jnp.zeros((6, slots), F32)], axis=0).astype(BF16)
    moved = jnp.dot(pair, pick_ref[...], preferred_element_type=F32)
    return 2.0 * moved[0:1] + moved[1:2]


def row_tables(j, points_ref, orders, near_ref, far_ref):
    slots = orders.shape[1]
    count = jnp.full((1, slots), points_ref[j], jnp.int32).astype(F32)
    row = iota((8, 1), 0)
    low_cos, low_sin = unit_circle(row.astype(F32), orders, count)
    mid_cos, mid_sin = unit_circle(16.0 * row.astype(F32), orders, count)
    far_cos, far_sin = unit_circle(128.0 * row.astype(F32), orders, count)
    step_cos, step_sin = unit_circle(jnp.where(row == 0, 8, 1024).astype(F32), orders, count)

    def twice(c, s, at):
        c1, s1 = step_cos[at:at + 1], step_sin[at:at + 1]
        return (jnp.concatenate([c, c * c1 - s * s1], axis=0),
                jnp.concatenate([s, c * s1 + s * c1], axis=0))

    fine_cos, fine_sin = twice(low_cos, low_sin, 0)
    far_cos, far_sin = twice(far_cos, far_sin, 1)
    weight = jnp.where(2.0 * orders >= count, 0.0, jnp.where(orders == 0.0, 1.0, 2.0))
    far_ref[j, 0] = far_cos * weight
    far_ref[j, 1] = far_sin * weight
    for i in range(slots // 128):
        own = slice(128 * i, 128 * (i + 1))
        c0, s0 = fine_cos[:, own], fine_sin[:, own]
        real, imag = [], []
        for b in range(8):
            c1, s1 = mid_cos[b:b + 1, own], mid_sin[b:b + 1, own]
            real.append(c1 * c0 - s1 * s0)
            imag.append(c1 * s0 + s1 * c0)
        near_ref[j, i] = jnp.concatenate(
            [jnp.concatenate(real, axis=0), jnp.concatenate(imag, axis=0)], axis=1
        ).astype(BF16)


def row_transform(j, near_ref, far_ref, rows_ref, pages_ref):
    blocks = rows_ref.shape[0]
    left = jnp.concatenate(
        [rows_ref[k1, pl.ds(j, 16, stride=4), :] for k1 in range(blocks)], axis=0
    ).astype(BF16)
    stacked = []
    for i in range(near_ref.shape[1]):
        own = slice(128 * i, 128 * (i + 1))
        partial = jnp.dot(left, near_ref[j, i], preferred_element_type=F32)
        total_real = jnp.zeros((16, 128), F32)
        total_imag = jnp.zeros((16, 128), F32)
        for k1 in range(blocks):
            u = partial[16 * k1:16 * (k1 + 1), :128]
            v = partial[16 * k1:16 * (k1 + 1), 128:]
            c2, s2 = far_ref[j, 0, k1:k1 + 1, own], far_ref[j, 1, k1:k1 + 1, own]
            total_real = total_real + (c2 * u - s2 * v)
            total_imag = total_imag + (c2 * v + s2 * u)
        stacked += [total_real, total_imag]
    pages_ref[:, j, :] = jnp.transpose(jnp.concatenate(stacked, axis=0))


def vertical_table(vert_ref):
    fields, levels, _ = vert_ref.shape
    spread = (iota((2 * levels, levels), 0) // 2 == iota((2 * levels, levels), 1)).astype(F32)
    rows = jnp.concatenate(
        [lax.dot_general(spread, vert_ref[f], NT, precision=lax.Precision.HIGHEST,
                         preferred_element_type=F32) for f in range(fields)], axis=0)
    column = iota((levels, 128), 1)
    pick = (iota((levels, 128), 0) == 4 * (column // 32) + column % 4).astype(F32)
    block = jnp.dot(rows, pick, precision=lax.Precision.HIGHEST, preferred_element_type=F32)
    shape = block.shape
    row, column = iota(shape, 0), iota(shape, 1)
    keep = (row // (2 * levels) == column // 4 % 4) & (row % 2 == column // 16 % 2)
    return jnp.where(keep, block, 0.0)


def finish(first_slot, order_ref, vert, joined_ref, table_ref, out_ref):
    high = vert.astype(BF16)
    low = (vert - high.astype(F32)).astype(BF16)
    halves = jnp.concatenate([high, low], axis=1)
    fields, levels = out_ref.shape[0], out_ref.shape[1]
    for i in range(4):
        block = joined_ref[i].astype(BF16)
        mixed = lax.dot_general(halves, jnp.concatenate([block, block], axis=1), NT,
                                preferred_element_type=F32)
        mixed_high = mixed.astype(BF16)
        mixed_low = (mixed - mixed_high.astype(F32)).astype(BF16)
        both = jnp.concatenate([mixed_high, mixed_low], axis=1)
        table = jnp.concatenate([table_ref[v, i] for v in range(4)], axis=0)
        table = jnp.concatenate([table, table], axis=1)
        summed = lax.dot_general(both, table, NT,
                                 preferred_element_type=F32)
        degree = iota(summed.shape, 1)
        summed = jnp.where(degree >= order_ref[first_slot + i], summed, 0.0)
        for q in range(fields * levels):
            out_ref[q // levels, q % levels, i] = summed[2 * q:2 * q + 2]


def kernel(waves, levs, grid_hbm, wind_hbm, points_hbm, order_hbm, orders_hbm, legendre_ref,
           vert_hbm, out_ref, grid_ref, wind_ref, points_ref, order_ref, orders_ref, vert_ref,
           pick_ref, near_ref, far_ref, rows_ref, pages_ref, send_ref, middle_ref, recv_ref,
           chunk_ref, joined_ref, table_ref,
           fetch_sem, wave_send_sem, wave_recv_sem, lev_send_sem, lev_recv_sem, table_send_sem,
           table_recv_sem, local_sem, near_sem):
    w, v = lax.axis_index("wave"), lax.axis_index("lev")
    me = w * levs + v
    fetches = [
        pltpu.make_async_copy(source, target, fetch_sem.at[at])
        for at, (source, target) in enumerate((
            (orders_hbm, orders_ref), (points_hbm, points_ref), (wind_hbm, wind_ref),
            (grid_hbm, grid_ref), (order_hbm, order_ref), (vert_hbm, vert_ref)))
    ]
    for fetch in fetches:
        fetch.start()
    own_table = pltpu.make_async_copy(
        legendre_ref.at[pl.ds(4 * v, 4)], table_ref.at[v], local_sem.at[5])
    own_table.start()

    planes, places = waves // 8, 8
    plane, place = w // places, lax.rem(w, places)
    mate = w + 1 - 2 * lax.rem(w, 2)
    along_y = [places * plane + lax.rem(place + 2 * step, places) for step in range(1, 4)]

    def others(first, last, action):
        def one(step, carry):
            target_plane = first + step // 6
            target = places * target_plane + lax.rem(
                2 * (place // 2) + 2 + lax.rem(step, 6), places)
            action(target, target_plane)
            return carry

        lax.fori_loop(0, 6 * (last - first), one, 0)

    greeted = plane - plane // 3
    last = plane + 1 + (3 - plane) // 2 * (planes - 1 - plane)
    barrier = pltpu.get_barrier_semaphore()

    def greet(target, lev):
        pl.semaphore_signal(barrier, inc=1, device_id=(target, lev), device_id_type=MESH)

    for step in range(1, levs):
        greet(w, lax.rem(v + step, levs))
    for step in range(planes):
        greet(lax.rem(mate + places * step, waves), v)
        if step > 0:
            greet(lax.rem(w + places * step, waves), v)
    others(plane, plane + 1, lambda target, _: greet(target, v))
    others(plane + 1, last, lambda target, _: greet(target, v))
    order_count = orders_ref.shape[1]
    column = iota((order_count, order_count), 1)
    pick_ref[...] = (iota((order_count, order_count), 0) == 16 * (column % 32) + 4 * (column // 32 % 4)
            + column // 128).astype(F32).astype(BF16)
    fetches[0].wait()
    fetches[1].wait()
    orders = column_orders(orders_ref, pick_ref)
    for j in range(4):
        row_tables(j, points_ref, orders, near_ref, far_ref)
    fetches[2].wait()
    fetches[3].wait()
    advect(grid_ref, wind_ref, points_ref, rows_ref)
    for j in range(4):
        row_transform(j, near_ref, far_ref, rows_ref, pages_ref)
    send_ref[...] = pages_ref[...].astype(BF16).reshape(send_ref.shape)
    table_copies = []

    def send_table(step, first, count):
        u = lax.rem(v + step, levs)
        at = len(table_copies)
        copy = pltpu.make_async_remote_copy(
            src_ref=legendre_ref.at[pl.ds(4 * u + first, count)],
            dst_ref=table_ref.at[v, pl.ds(first, count)],
            send_sem=table_send_sem.at[at], recv_sem=table_recv_sem.at[at],
            device_id=(w, u), device_id_type=MESH)
        copy.start()
        table_copies.append(copy)

    own_pages = pltpu.make_async_copy(send_ref.at[:, w], middle_ref.at[:, w], wave_recv_sem.at[0])
    own_pages.start()
    pl.semaphore_wait(barrier, levs - 1 + 2 * planes - 1 + 6 + 6 * greeted)
    for target in along_y:
        pl.semaphore_signal(near_sem, inc=1, device_id=(target, v), device_id_type=MESH)

    def send(target, target_plane):
        turn = lax.rem(target_plane + planes - plane, planes)
        pltpu.make_async_remote_copy(
            src_ref=send_ref.at[:, target], dst_ref=middle_ref.at[:, w],
            send_sem=wave_send_sem, recv_sem=wave_recv_sem.at[turn],
            device_id=(target, v), device_id_type=MESH,
        ).start()

    others(0, greeted, send)
    for step in (2, 1, 3, 0):
        target_plane = lax.rem(plane + step, planes)
        send(lax.rem(mate + places * step, waves), target_plane)
        if step > 0:
            send(lax.rem(w + places * step, waves), target_plane)
    others(plane, plane + 1, send)
    send_table(1, 0, 4)
    send_table(3, 0, 4)
    pl.semaphore_wait(near_sem, len(along_y))
    others(greeted, plane, send)
    others(plane + 1, planes, send)
    send_table(2, 0, 4)
    fetches[4].wait()
    fetches[5].wait()
    vert = vertical_table(vert_ref)
    partner = {"device_id": (mate, v), "device_id_type": MESH}
    lev_copies, own_blocks = [], []
    arrived = middle_ref.at[:, pl.ds(0, places)]
    for source in range(planes):
        turn = lax.rem(plane + planes - source, planes)
        pltpu.make_async_remote_copy(
            src_ref=arrived, dst_ref=arrived, send_sem=wave_send_sem,
            recv_sem=wave_recv_sem.at[turn], **partner).wait_recv()
        part = pl.ds(places * source, places)
        for step in (2, 1, 3):
            u = lax.rem(v + step, levs)
            at = 3 * source + step - 1
            copy = pltpu.make_async_remote_copy(
                src_ref=middle_ref.at[u, part], dst_ref=recv_ref.at[v, part],
                send_sem=lev_send_sem.at[at], recv_sem=lev_recv_sem.at[at],
                device_id=(w, u), device_id_type=MESH)
            copy.start()
            lev_copies.append(copy)
        copy = pltpu.make_async_copy(
            middle_ref.at[v, part], recv_ref.at[v, part], local_sem.at[source])
        copy.start()
        own_blocks.append(copy)
    own_table.wait()
    for copy in table_copies:
        copy.wait_recv()
    for source in range(planes):
        for copy in lev_copies[3 * source:3 * source + 3]:
            copy.wait_recv()
        own_blocks[source].wait()
        chunks = []
        for lev in range(levs):
            for at in range(places):
                row = 4 * (places * lev + at)
                chunk_ref[row:row + 4, :] = recv_ref[lev, places * source + at].astype(F32)
            chunks.append(chunk_ref[4 * places * lev:4 * places * (lev + 1), :])
        for i in range(4):
            joined_ref[i, 4 * places * source:4 * places * (source + 1), :] = jnp.concatenate(
                [chunk[:, 32 * i:32 * (i + 1)] for chunk in chunks], axis=1)
    finish(4 * me, order_ref, vert, joined_ref, table_ref, out_ref)
    for copy in table_copies + lev_copies:
        copy.wait_send()
    left = send_ref.at[:, pl.ds(0, waves - 1)]
    pltpu.make_async_remote_copy(
        src_ref=left, dst_ref=left, send_sem=wave_send_sem, recv_sem=wave_recv_sem.at[0],
        **partner).wait_send()


def body(grid_adjoint, courant, row_points, wave_order, legendre, vert_inverse, *, waves, levs):
    fields, levels, rows, width = grid_adjoint.shape
    slots = legendre.shape[0] // levs
    degrees = legendre.shape[1] * levs
    orders = wave_order.reshape(1, -1)
    hbm = pl.BlockSpec(memory_space=pltpu.HBM)
    return pl.pallas_call(
        functools.partial(kernel, waves, levs),
        out_shape=pltpu.VMEM((fields, levels * levs, slots, 2, degrees), F32),
        in_specs=[hbm] * 7,
        out_specs=pl.BlockSpec(memory_space=pltpu.VMEM),
        scratch_shapes=[
            pltpu.VMEM(grid_adjoint.shape, BF16),
            pltpu.VMEM(courant.shape, BF16),
            pltpu.SMEM(row_points.shape, jnp.int32),
            pltpu.SMEM(wave_order.shape, jnp.int32),
            pltpu.VMEM(orders.shape, jnp.int32),
            pltpu.VMEM(vert_inverse.shape, F32),
            pltpu.VMEM((512, 512), BF16),
            pltpu.VMEM((rows, 4, 128, 256), BF16),
            pltpu.VMEM((rows, 2, 16, 512), F32),
            pltpu.VMEM((width // 128, 64, 128), F32),
            pltpu.VMEM((waves * levs, rows, 128), F32),
            pltpu.VMEM((levs, waves, rows, 128), BF16),
            pltpu.VMEM((levs, waves, rows, 128), BF16),
            pltpu.VMEM((levs, waves, rows, 128), BF16),
            pltpu.VMEM((levs * 8 * rows, 128), F32),
            pltpu.VMEM((slots, waves * rows, 128), F32),
            pltpu.VMEM((levs, slots) + legendre.shape[1:], BF16),
            pltpu.SemaphoreType.DMA((6,)),
            pltpu.SemaphoreType.DMA,
            pltpu.SemaphoreType.DMA((4,)),
            pltpu.SemaphoreType.DMA((12,)),
            pltpu.SemaphoreType.DMA((12,)),
            pltpu.SemaphoreType.DMA((8,)),
            pltpu.SemaphoreType.DMA((8,)),
            pltpu.SemaphoreType.DMA((6,)),
            pltpu.SemaphoreType.REGULAR,
        ],
        compiler_params=pltpu.CompilerParams(
            collective_id=0, has_side_effects=True, vmem_limit_bytes=56 * 2**20),
    )(grid_adjoint, courant, row_points, wave_order, orders, legendre, vert_inverse)


def solution(mesh):
    return jax.shard_map(
        functools.partial(body, waves=mesh.shape["wave"], levs=mesh.shape["lev"]),
        mesh=mesh,
        in_specs=(
            P(None, "lev", "wave", None),
            P("lev", "wave", None),
            P("wave"),
            P(),
            P("wave", "lev", None),
            P(),
        ),
        out_specs=P(None, None, ("wave", "lev"), None, None),
        check_vma=False,
    )
```

```python
import functools

import jax
import jax.numpy as jnp
from jax import lax
from jax.experimental import pallas as pl
from jax.experimental.pallas import tpu as pltpu
from jax.sharding import PartitionSpec as P

F32 = jnp.float32
BF16 = jnp.bfloat16
MESH = pl.DeviceIdType.MESH
NT = (((1,), (1,)), ((), ()))

SIN_PI = (3.1415927410125732, -5.167712688446045, 2.5501632690429688,
          -0.5992521643638611, 0.08205024898052216, -0.007028118707239628)
COS_PI = (1.0, -4.934802055358887, 4.058709144592285,
          -1.3352118730545044, 0.2349366992712021, -0.024395223706960678)


def horner(coefficients, z):
    value = jnp.full(z.shape, coefficients[-1], F32)
    for c in coefficients[-2::-1]:
        value = value * z + c
    return value


def unit_circle(steps, orders, count):
    inverse = 1.0 / count
    product = steps * orders
    turns = jnp.floor(product * inverse + 0.5)
    x = (product - turns * count) * inverse
    z = x * x
    s = x * horner(SIN_PI, z)
    c = horner(COS_PI, z)
    return 1.0 - 2.0 * s * s, -2.0 * s * c


def iota(shape, axis):
    return lax.broadcasted_iota(jnp.int32, shape, axis)


def advect(grid_ref, wind_ref, points_ref, rows_ref):
    fields, levels, rows, width = grid_ref.shape
    shape = (2 * rows, width)
    row = iota(shape, 0) % rows
    count = jnp.full(shape, points_ref[0], jnp.int32)
    for j in range(1, rows):
        count = jnp.where(row == j, points_ref[j], count)
    position = iota(shape, 1)
    inside = position < count
    at_end = position == count - 1
    at_start = position == 0

    def pair(ref, *at):
        return jnp.concatenate(
            [ref[(*at[:-1], at[-1] + half)].astype(F32) for half in range(2)], axis=0)

    for level in range(0, levels, 2):
        wind = pair(wind_ref, level)
        for field in range(fields):
            grid = pair(grid_ref, field, level)
            flux = jnp.where(inside, wind * grid, 0.0)
            first = flux[:, :1]
            last = jnp.sum(jnp.where(at_end, flux, 0.0), axis=1, keepdims=True)
            forward = jnp.where(at_end, first, pltpu.roll(flux, width - 1, 1))
            backward = jnp.where(at_start, last, pltpu.roll(flux, 1, 1))
            result = jnp.where(inside, grid + 0.5 * (forward - backward), 0.0)
            at = rows * (field * levels + level)
            for k1 in range(width // 128):
                rows_ref[k1, at:at + 2 * rows, :] = result[:, 128 * k1:128 * (k1 + 1)]
    used = rows * fields * levels
    rows_ref[:, used:, :] = jnp.zeros((rows_ref.shape[0], rows_ref.shape[1] - used, 128), F32)


def column_orders(orders_ref, pick_ref):
    slots = orders_ref.shape[1]
    orders = orders_ref[...].astype(F32)
    high = jnp.floor(orders * 0.5)
    low = orders - 2.0 * high
    pair = jnp.concatenate([high, low, jnp.zeros((6, slots), F32)], axis=0).astype(BF16)
    moved = jnp.dot(pair, pick_ref[...], preferred_element_type=F32)
    return 2.0 * moved[0:1] + moved[1:2]


def row_tables(j, points_ref, orders, near_ref, far_ref):
    slots = orders.shape[1]
    count = jnp.full((1, slots), points_ref[j], jnp.int32).astype(F32)
    row = iota((8, 1), 0)
    low_cos, low_sin = unit_circle(row.astype(F32), orders, count)
    mid_cos, mid_sin = unit_circle(16.0 * row.astype(F32), orders, count)
    far_cos, far_sin = unit_circle(128.0 * row.astype(F32), orders, count)
    step_cos, step_sin = unit_circle(jnp.where(row == 0, 8, 1024).astype(F32), orders, count)

    def twice(c, s, at):
        c1, s1 = step_cos[at:at + 1], step_sin[at:at + 1]
        return (jnp.concatenate([c, c * c1 - s * s1], axis=0),
                jnp.concatenate([s, c * s1 + s * c1], axis=0))

    fine_cos, fine_sin = twice(low_cos, low_sin, 0)
    far_cos, far_sin = twice(far_cos, far_sin, 1)
    weight = jnp.where(2.0 * orders >= count, 0.0, jnp.where(orders == 0.0, 1.0, 2.0))
    far_ref[j, 0] = far_cos * weight
    far_ref[j, 1] = far_sin * weight
    for i in range(slots // 128):
        own = slice(128 * i, 128 * (i + 1))
        c0, s0 = fine_cos[:, own], fine_sin[:, own]
        real, imag = [], []
        for b in range(8):
            c1, s1 = mid_cos[b:b + 1, own], mid_sin[b:b + 1, own]
            real.append(c1 * c0 - s1 * s0)
            imag.append(c1 * s0 + s1 * c0)
        near_ref[j, i] = jnp.concatenate(
            [jnp.concatenate(real, axis=0), jnp.concatenate(imag, axis=0)], axis=1
        ).astype(BF16)


def row_transform(j, near_ref, far_ref, rows_ref, pages_ref):
    blocks = rows_ref.shape[0]
    left = jnp.concatenate(
        [rows_ref[k1, pl.ds(j, 16, stride=4), :] for k1 in range(blocks)], axis=0
    ).astype(BF16)
    stacked = []
    for i in range(near_ref.shape[1]):
        own = slice(128 * i, 128 * (i + 1))
        partial = jnp.dot(left, near_ref[j, i], preferred_element_type=F32)
        total_real = jnp.zeros((16, 128), F32)
        total_imag = jnp.zeros((16, 128), F32)
        for k1 in range(blocks):
            u = partial[16 * k1:16 * (k1 + 1), :128]
            v = partial[16 * k1:16 * (k1 + 1), 128:]
            c2, s2 = far_ref[j, 0, k1:k1 + 1, own], far_ref[j, 1, k1:k1 + 1, own]
            total_real = total_real + (c2 * u - s2 * v)
            total_imag = total_imag + (c2 * v + s2 * u)
        stacked += [total_real, total_imag]
    pages_ref[:, j, :] = jnp.transpose(jnp.concatenate(stacked, axis=0))


def vertical_table(vert_ref):
    fields, levels, _ = vert_ref.shape
    spread = (iota((2 * levels, levels), 0) // 2 == iota((2 * levels, levels), 1)).astype(F32)
    rows = jnp.concatenate(
        [lax.dot_general(spread, vert_ref[f], NT, precision=lax.Precision.HIGHEST,
                         preferred_element_type=F32) for f in range(fields)], axis=0)
    column = iota((levels, 128), 1)
    pick = (iota((levels, 128), 0) == 4 * (column // 32) + column % 4).astype(F32)
    block = jnp.dot(rows, pick, precision=lax.Precision.HIGHEST, preferred_element_type=F32)
    shape = block.shape
    row, column = iota(shape, 0), iota(shape, 1)
    keep = (row // (2 * levels) == column // 4 % 4) & (row % 2 == column // 16 % 2)
    return jnp.where(keep, block, 0.0)


def finish(first_slot, order_ref, vert, joined_ref, table_ref, out_ref):
    high = vert.astype(BF16)
    low = (vert - high.astype(F32)).astype(BF16)
    halves = jnp.concatenate([high, low], axis=1)
    fields, levels = out_ref.shape[0], out_ref.shape[1]
    slots, rows, width = joined_ref.shape
    block = joined_ref[...].reshape(slots * rows, width).astype(BF16)
    mixed = lax.dot_general(halves, jnp.concatenate([block, block], axis=1), NT,
                            preferred_element_type=F32)
    mixed_high = mixed.astype(BF16)
    mixed_low = (mixed - mixed_high.astype(F32)).astype(BF16)
    for i in range(slots):
        own = slice(rows * i, rows * (i + 1))
        both = jnp.concatenate([mixed_high[:, own], mixed_low[:, own]], axis=1)
        table = jnp.concatenate([table_ref[v, i] for v in range(4)], axis=0)
        table = jnp.concatenate([table, table], axis=1)
        summed = lax.dot_general(both, table, NT,
                                 preferred_element_type=F32)
        degree = iota(summed.shape, 1)
        summed = jnp.where(degree >= order_ref[first_slot + i], summed, 0.0)
        for q in range(fields * levels):
            out_ref[q // levels, q % levels, i] = summed[2 * q:2 * q + 2]


def kernel(waves, levs, grid_hbm, wind_hbm, points_hbm, order_hbm, orders_hbm, legendre_ref,
           vert_hbm, out_ref, grid_ref, wind_ref, points_ref, order_ref, orders_ref, vert_ref,
           pick_ref, near_ref, far_ref, rows_ref, pages_ref, send_ref, middle_ref, recv_ref,
           chunk_ref, joined_ref, table_ref,
           fetch_sem, wave_send_sem, wave_recv_sem, lev_send_sem, lev_recv_sem, table_send_sem,
           table_recv_sem, local_sem, near_sem):
    w, v = lax.axis_index("wave"), lax.axis_index("lev")
    me = w * levs + v
    fetches = [
        pltpu.make_async_copy(source, target, fetch_sem.at[at])
        for at, (source, target) in enumerate((
            (orders_hbm, orders_ref), (points_hbm, points_ref), (wind_hbm, wind_ref),
            (grid_hbm, grid_ref), (order_hbm, order_ref), (vert_hbm, vert_ref)))
    ]
    for fetch in fetches:
        fetch.start()
    own_table = pltpu.make_async_copy(
        legendre_ref.at[pl.ds(4 * v, 4)], table_ref.at[v], local_sem.at[5])
    own_table.start()

    planes, places = waves // 8, 8
    plane, place = w // places, lax.rem(w, places)
    mate = w + 1 - 2 * lax.rem(w, 2)
    along_y = [places * plane + lax.rem(place + 2 * step, places) for step in range(1, 4)]

    def others(first, last, action):
        def one(step, carry):
            target_plane = first + step // 6
            target = places * target_plane + lax.rem(
                2 * (place // 2) + 2 + lax.rem(step, 6), places)
            action(target, target_plane)
            return carry

        lax.fori_loop(0, 6 * (last - first), one, 0)

    greeted = plane - plane // 3
    last = plane + 1 + (3 - plane) // 2 * (planes - 1 - plane)
    barrier = pltpu.get_barrier_semaphore()

    def greet(target, lev):
        pl.semaphore_signal(barrier, inc=1, device_id=(target, lev), device_id_type=MESH)

    for step in range(1, levs):
        greet(w, lax.rem(v + step, levs))
    for step in range(planes):
        greet(lax.rem(mate + places * step, waves), v)
        if step > 0:
            greet(lax.rem(w + places * step, waves), v)
    others(plane, plane + 1, lambda target, _: greet(target, v))
    others(plane + 1, last, lambda target, _: greet(target, v))
    order_count = orders_ref.shape[1]
    column = iota((order_count, order_count), 1)
    pick_ref[...] = (iota((order_count, order_count), 0) == 16 * (column % 32) + 4 * (column // 32 % 4)
            + column // 128).astype(F32).astype(BF16)
    fetches[0].wait()
    fetches[1].wait()
    orders = column_orders(orders_ref, pick_ref)
    for j in range(4):
        row_tables(j, points_ref, orders, near_ref, far_ref)
    fetches[2].wait()
    fetches[3].wait()
    advect(grid_ref, wind_ref, points_ref, rows_ref)
    for j in range(4):
        row_transform(j, near_ref, far_ref, rows_ref, pages_ref)
    send_ref[...] = pages_ref[...].astype(BF16).reshape(send_ref.shape)
    table_copies = []

    def send_table(step, first, count):
        u = lax.rem(v + step, levs)
        at = len(table_copies)
        copy = pltpu.make_async_remote_copy(
            src_ref=legendre_ref.at[pl.ds(4 * u + first, count)],
            dst_ref=table_ref.at[v, pl.ds(first, count)],
            send_sem=table_send_sem.at[at], recv_sem=table_recv_sem.at[at],
            device_id=(w, u), device_id_type=MESH)
        copy.start()
        table_copies.append(copy)

    own_pages = pltpu.make_async_copy(send_ref.at[:, w], middle_ref.at[:, w], wave_recv_sem.at[0])
    own_pages.start()
    pl.semaphore_wait(barrier, levs - 1 + 2 * planes - 1 + 6 + 6 * greeted)
    for target in along_y:
        pl.semaphore_signal(near_sem, inc=1, device_id=(target, v), device_id_type=MESH)

    def send(target, target_plane):
        turn = lax.rem(target_plane + planes - plane, planes)
        pltpu.make_async_remote_copy(
            src_ref=send_ref.at[:, target], dst_ref=middle_ref.at[:, w],
            send_sem=wave_send_sem, recv_sem=wave_recv_sem.at[turn],
            device_id=(target, v), device_id_type=MESH,
        ).start()

    others(0, greeted, send)
    for step in (2, 1, 3, 0):
        target_plane = lax.rem(plane + step, planes)
        send(lax.rem(mate + places * step, waves), target_plane)
        if step > 0:
            send(lax.rem(w + places * step, waves), target_plane)
    others(plane, plane + 1, send)
    send_table(1, 0, 4)
    send_table(3, 0, 4)
    pl.semaphore_wait(near_sem, len(along_y))
    others(greeted, plane, send)
    others(plane + 1, planes, send)
    send_table(2, 0, 4)
    fetches[4].wait()
    fetches[5].wait()
    vert = vertical_table(vert_ref)
    partner = {"device_id": (mate, v), "device_id_type": MESH}
    lev_copies, own_blocks = [], []
    arrived = middle_ref.at[:, pl.ds(0, places)]
    for source in range(planes):
        turn = lax.rem(plane + planes - source, planes)
        pltpu.make_async_remote_copy(
            src_ref=arrived, dst_ref=arrived, send_sem=wave_send_sem,
            recv_sem=wave_recv_sem.at[turn], **partner).wait_recv()
        part = pl.ds(places * source, places)
        for step in (2, 1, 3):
            u = lax.rem(v + step, levs)
            at = 3 * source + step - 1
            copy = pltpu.make_async_remote_copy(
                src_ref=middle_ref.at[u, part], dst_ref=recv_ref.at[v, part],
                send_sem=lev_send_sem.at[at], recv_sem=lev_recv_sem.at[at],
                device_id=(w, u), device_id_type=MESH)
            copy.start()
            lev_copies.append(copy)
        copy = pltpu.make_async_copy(
            middle_ref.at[v, part], recv_ref.at[v, part], local_sem.at[source])
        copy.start()
        own_blocks.append(copy)
    own_table.wait()
    for copy in table_copies:
        copy.wait_recv()
    for source in range(planes):
        for copy in lev_copies[3 * source:3 * source + 3]:
            copy.wait_recv()
        own_blocks[source].wait()
        chunks = []
        for lev in range(levs):
            for at in range(places):
                row = 4 * (places * lev + at)
                chunk_ref[row:row + 4, :] = recv_ref[lev, places * source + at].astype(F32)
            chunks.append(chunk_ref[4 * places * lev:4 * places * (lev + 1), :])
        for i in range(4):
            joined_ref[i, 4 * places * source:4 * places * (source + 1), :] = jnp.concatenate(
                [chunk[:, 32 * i:32 * (i + 1)] for chunk in chunks], axis=1)
    finish(4 * me, order_ref, vert, joined_ref, table_ref, out_ref)
    for copy in table_copies + lev_copies:
        copy.wait_send()
    left = send_ref.at[:, pl.ds(0, waves - 1)]
    pltpu.make_async_remote_copy(
        src_ref=left, dst_ref=left, send_sem=wave_send_sem, recv_sem=wave_recv_sem.at[0],
        **partner).wait_send()


def body(grid_adjoint, courant, row_points, wave_order, legendre, vert_inverse, *, waves, levs):
    fields, levels, rows, width = grid_adjoint.shape
    slots = legendre.shape[0] // levs
    degrees = legendre.shape[1] * levs
    orders = wave_order.reshape(1, -1)
    hbm = pl.BlockSpec(memory_space=pltpu.HBM)
    return pl.pallas_call(
        functools.partial(kernel, waves, levs),
        out_shape=pltpu.VMEM((fields, levels * levs, slots, 2, degrees), F32),
        in_specs=[hbm] * 7,
        out_specs=pl.BlockSpec(memory_space=pltpu.VMEM),
        scratch_shapes=[
            pltpu.VMEM(grid_adjoint.shape, BF16),
            pltpu.VMEM(courant.shape, BF16),
            pltpu.SMEM(row_points.shape, jnp.int32),
            pltpu.SMEM(wave_order.shape, jnp.int32),
            pltpu.VMEM(orders.shape, jnp.int32),
            pltpu.VMEM(vert_inverse.shape, F32),
            pltpu.VMEM((512, 512), BF16),
            pltpu.VMEM((rows, 4, 128, 256), BF16),
            pltpu.VMEM((rows, 2, 16, 512), F32),
            pltpu.VMEM((width // 128, 64, 128), F32),
            pltpu.VMEM((waves * levs, rows, 128), F32),
            pltpu.VMEM((levs, waves, rows, 128), BF16),
            pltpu.VMEM((levs, waves, rows, 128), BF16),
            pltpu.VMEM((levs, waves, rows, 128), BF16),
            pltpu.VMEM((levs * 8 * rows, 128), F32),
            pltpu.VMEM((slots, waves * rows, 128), F32),
            pltpu.VMEM((levs, slots) + legendre.shape[1:], BF16),
            pltpu.SemaphoreType.DMA((6,)),
            pltpu.SemaphoreType.DMA,
            pltpu.SemaphoreType.DMA((4,)),
            pltpu.SemaphoreType.DMA((12,)),
            pltpu.SemaphoreType.DMA((12,)),
            pltpu.SemaphoreType.DMA((8,)),
            pltpu.SemaphoreType.DMA((8,)),
            pltpu.SemaphoreType.DMA((6,)),
            pltpu.SemaphoreType.REGULAR,
        ],
        compiler_params=pltpu.CompilerParams(
            collective_id=0, has_side_effects=True, vmem_limit_bytes=56 * 2**20),
    )(grid_adjoint, courant, row_points, wave_order, orders, legendre, vert_inverse)


def solution(mesh):
    return jax.shard_map(
        functools.partial(body, waves=mesh.shape["wave"], levs=mesh.shape["lev"]),
        mesh=mesh,
        in_specs=(
            P(None, "lev", "wave", None),
            P("lev", "wave", None),
            P("wave"),
            P(),
            P("wave", "lev", None),
            P(),
        ),
        out_specs=P(None, None, ("wave", "lev"), None, None),
        check_vma=False,
    )
```
